32 devices in a mesh: tgt: 8 (over y, x, core), src: 4 (over z).
Axes of the slice: x: 2, y: 2, z: 4, core: 2. Of those that a mesh axis runs over, the one named last changes fastest.
Arguments:
- incident: bfloat16 [128, 8, 2048], P(None, None, 'tgt'), may hold values from -6 to 6
- past_density: bfloat16 [76, 8, 2048], P(None, None, 'src'), may hold values from -6 to 6
- kernels: bfloat16 [8, 2048, 2048], P(None, 'src', 'tgt'), may hold values from -0.0625 to 0.0625
- lag_offset: int32 [8, 4, 12], P('tgt', 'src'), may hold values from 0 to 11, each once within a row
- lag_counts: int32 [8, 4], P('tgt', 'src'), may hold values from 2 to 8, as said below
- couplings: float32 [2, 2048, 256], P(None, 'tgt'), may hold values from -0.86 to 0.01
- inverse: float32 [2048, 256], P('tgt'), may hold values from -0.02 to 1.06
Outputs:
- densities: float32 [128, 8, 2048], P(None, None, 'tgt')
The draws below stay inside these ranges and needn't reach their ends.
Inputs may be any that keep to these rules, and one draw needn't show every extreme that they name: `lag_counts`: each tile has between 2 and 8 nonzero retarded lags; in every draw some tile has 8.
All inputs are finite; a program needn't handle non-finite values.
Results may differ from the reference program's by a relative error of at most 0.0014.
Values may be sent and summed in bfloat16 or wider, within the bound.
No kernel may reach another device: no remote copies, remote signals or barrier semaphores. Data moves between devices by JAX's collectives and lax.ppermute only.
A program may use at most 64 MiB of HBM per device.

```python
import math
import jax
import jax.numpy as jnp
from jax import lax

ROW_DEV = 256
TGT_GROUPS = 8
SRC_GROUPS = 4
COL_DEV = 512
M = 2048
LOADS = 8
BLOCK_STEPS = 64
BLOCKS = 2
STEPS = 128
SLOTS = 8
LAG_SPAN = 12
HIST = 76
COUPLINGS = 2


def draw_lag_counts(key, part):
    light_key, heavy_key, spot_key = jax.random.split(jax.random.fold_in(key, 11), 3)
    light_load = jax.random.randint(light_key, (TGT_GROUPS, SRC_GROUPS), 2, 5)
    heavy_tile = jax.random.randint(heavy_key, (TGT_GROUPS, SRC_GROUPS), 0, 8) == 0
    values = jnp.where(heavy_tile, SLOTS, light_load).reshape(-1)
    chosen = jax.random.randint(spot_key, (), 0, TGT_GROUPS * SRC_GROUPS)
    values = values.at[chosen].set(SLOTS)
    return values.reshape(TGT_GROUPS, SRC_GROUPS).astype(jnp.int32)


def group_identity():
    within_group = jnp.arange(M) % ROW_DEV
    return (within_group[:, None] == jnp.arange(ROW_DEV)[None, :]).astype(jnp.float32)


def draw_couplings(key, part):
    rate_key, first_key, second_key = jax.random.split(jax.random.fold_in(key, 31), 3)
    forget = jnp.exp(jax.random.uniform(rate_key, (M,), jnp.float32, math.log(0.15), math.log(0.8)))
    retain = 1.0 - forget
    first_noise = jax.random.truncated_normal(first_key, -4.0, 4.0, (M, ROW_DEV), jnp.float32)
    second_noise = jax.random.truncated_normal(second_key, -4.0, 4.0, (M, ROW_DEV), jnp.float32)
    first = -retain[:, None] * group_identity() + 0.01 * first_noise / math.sqrt(ROW_DEV)
    second = 0.01 * second_noise / math.sqrt(ROW_DEV)
    stacked = [first, second]
    for extra in range(2, COUPLINGS):
        stacked.append(0.01 * jax.random.truncated_normal(jax.random.fold_in(second_key, extra), -4.0, 4.0, (M, ROW_DEV), jnp.float32) / math.sqrt(ROW_DEV))
    return jnp.stack(stacked[:COUPLINGS], 0)


def draw_inverse(key, part):
    noise_part = jax.random.truncated_normal(jax.random.fold_in(key, 23), -4.0, 4.0, (M, ROW_DEV), jnp.float32)
    gains = jax.random.uniform(jax.random.fold_in(key, 29), (M,), jnp.float32, 0.7, 1.05)
    return gains[:, None] * group_identity() + 0.015 * noise_part / math.sqrt(ROW_DEV)


def block_levels(stream_key, shape, cuts, least, largest):
    factor_of = 1.0
    for axis_at, parts in cuts:
        draws = jax.random.uniform(jax.random.fold_in(jax.random.fold_in(stream_key, 6), axis_at), (parts,), jnp.float32, least / len(cuts), largest / len(cuts))
        factor_of = factor_of * jnp.repeat(jnp.exp(draws), shape[axis_at] // parts).reshape((-1,) + (1,) * (len(shape) - 1 - axis_at))
    return factor_of


def noise(own_key, extent, deviation, limit, shards=(), kind=jnp.bfloat16):
    array = jax.random.normal(own_key, extent, jnp.float32) * deviation
    if len(shards) > 0:
        array = block_levels(own_key, extent, shards, -0.22, 0.18) * array
    return jnp.clip(array, min=-limit, max=limit).astype(kind)


def setup_inputs(seed: int = 0) -> dict:
    splits = jax.random.split(jax.random.key(seed), 8)
    return {
        "incident": noise(splits[0], (STEPS, LOADS, M), 1.0, 6.0, ((2, 8),)),
        "past_density": noise(splits[1], (HIST, LOADS, M), 1.0, 6.0, ((2, 4),)),
        "kernels": noise(splits[2], (SLOTS, M, M), (M * 4) ** -0.5, 0.0625, ((1, 4), (2, 8))),
        "lag_offset": jax.vmap(lambda own: jax.random.permutation(own, LAG_SPAN))(jax.random.split(splits[3], TGT_GROUPS * SRC_GROUPS)).reshape((TGT_GROUPS, SRC_GROUPS, LAG_SPAN)).astype(jnp.int32),
        "lag_counts": draw_lag_counts(jax.random.fold_in(splits[7], 71), 0),
        "couplings": draw_couplings(jax.random.fold_in(splits[7], 71), 0),
        "inverse": draw_inverse(jax.random.fold_in(splits[7], 71), 0),
    }


precise = lax.Precision.HIGHEST


def far_block(kernels, lag_offset, lag_counts, history, first_step):
    def per_target(target):
        def per_source(source, running):
            source = source.astype(jnp.int32)

            def per_slot(slot_index, partial_sum):
                slot_index = slot_index.astype(jnp.int32)
                lag_value = (BLOCK_STEPS + lag_offset[target, source, slot_index]).astype(jnp.int32)
                window = lax.dynamic_slice(history, ((first_step + HIST - lag_value).astype(jnp.int32), jnp.int32(0), (source * COL_DEV).astype(jnp.int32)), (BLOCK_STEPS, LOADS, COL_DEV))
                kernel_block = lax.dynamic_slice(kernels, (slot_index, (source * COL_DEV).astype(jnp.int32), (target * ROW_DEV).astype(jnp.int32)), (1, COL_DEV, ROW_DEV))[0]
                return partial_sum + jnp.dot(window.reshape(BLOCK_STEPS * LOADS, COL_DEV), kernel_block, preferred_element_type=jnp.float32)

            return lax.fori_loop(jnp.int32(0), lag_counts[target, source].astype(jnp.int32), per_slot, running)

        initial = jnp.zeros((BLOCK_STEPS * LOADS, ROW_DEV), jnp.float32)
        return lax.fori_loop(jnp.int32(0), jnp.int32(SRC_GROUPS), per_source, initial)

    stacked = lax.map(per_target, jnp.arange(TGT_GROUPS, dtype=jnp.int32))
    return stacked.reshape(TGT_GROUPS, BLOCK_STEPS, LOADS, ROW_DEV).transpose(1, 2, 0, 3).reshape(BLOCK_STEPS, LOADS, M)


def self_block(driving, earlier, couplings, inverse):
    grouped_couplings = couplings.reshape(COUPLINGS, TGT_GROUPS, ROW_DEV, ROW_DEV)
    grouped_inverse = inverse.reshape(TGT_GROUPS, ROW_DEV, ROW_DEV)

    def within_groups(vector_rows, matrices):
        split_rows = vector_rows.reshape(LOADS, TGT_GROUPS, ROW_DEV)
        return jnp.einsum("lgr,grk->lgk", split_rows, matrices, precision=precise).reshape(LOADS, M)

    def advance(earlier_steps, driving_step):
        adjusted = driving_step
        for shift_lag in range(1, COUPLINGS + 1):
            adjusted = adjusted - within_groups(earlier_steps[COUPLINGS - shift_lag], grouped_couplings[shift_lag - 1])
        solved = within_groups(adjusted, grouped_inverse)
        return jnp.concatenate([earlier_steps[1:], solved[None]], 0), solved

    return lax.scan(advance, earlier, driving)


def reference(incident, past_density, kernels, lag_offset, lag_counts, couplings, inverse):
    history = jnp.concatenate([past_density, jnp.zeros((STEPS, LOADS, M), jnp.bfloat16)], 0)
    earlier = past_density[HIST - COUPLINGS:].astype(jnp.float32)
    produced = []
    for block_index in range(BLOCKS):
        first_step = block_index * BLOCK_STEPS
        far_field = far_block(kernels, lag_offset, lag_counts, history, first_step)
        driving = incident[first_step:first_step + BLOCK_STEPS].astype(jnp.float32) - far_field
        earlier, solved = self_block(driving, earlier, couplings, inverse)
        produced.append(solved)
        history = history.at[HIST + first_step:HIST + first_step + BLOCK_STEPS].set(solved.astype(jnp.bfloat16))
    return jnp.concatenate(produced, 0)
```

```python
import functools

import jax
import jax.numpy as jnp
from jax import lax
from jax.experimental import pallas as pl
from jax.experimental.pallas import tpu as pltpu
from jax.sharding import PartitionSpec as P

F32 = jnp.float32
BF16 = jnp.bfloat16
LANES = 128
SUBLANES = 8
VMEM = pl.BlockSpec(memory_space=pltpu.VMEM)
SMEM = pl.BlockSpec(memory_space=pltpu.SMEM)
ANY = pl.BlockSpec(memory_space=pl.ANY)


def partner(index, shift, count):
    if count & (count - 1) == 0:
        return index ^ shift
    return (index + shift) % count


def sender(index, shift, count):
    if count & (count - 1) == 0:
        return index ^ shift
    return (index - shift) % count


def split(value):
    high = value.astype(BF16)
    return high, (value - high.astype(F32)).astype(BF16)


def dot3(value, high, low):
    rows = value.shape[0]
    value_high, value_low = split(value)
    both = jnp.dot(
        jnp.concatenate([value_high, value_low], 0), high, preferred_element_type=F32
    )
    cross = jnp.dot(value_high, low, preferred_element_type=F32)
    return both[:rows] + (both[rows:] + cross)


def sum_slots(ints, window_of, kernels, kernel_buffer, sems, total, span):
    count = ints[0]
    slots = kernel_buffer.shape[0]

    def fetch(slot):
        return pltpu.make_async_copy(
            kernels.at[slot], kernel_buffer.at[slot], sems.at[slot]
        )

    total[...] = jnp.zeros_like(total)

    def add(slot, carry):
        fetch(slot).wait()
        window = window_of(span - ints[1 + slot])
        total[...] += jnp.dot(
            window, kernel_buffer[slot], preferred_element_type=F32
        )
        return carry

    lax.fori_loop(0, count, add, 0)


def start_slots(ints, kernels, kernel_buffer, sems):
    for slot in range(kernel_buffer.shape[0]):

        @pl.when(slot < ints[0])
        def _():
            pltpu.make_async_copy(
                kernels.at[slot], kernel_buffer.at[slot], sems.at[slot]
            ).start()


def split_loads(total, strided, by_load, loads, steps):
    groups = strided.shape[0]
    for group in range(groups):
        strided[group] = total[:, group * LANES : (group + 1) * LANES]
    for load in range(loads):
        for group in range(groups):
            by_load[load, :, group * LANES : (group + 1) * LANES] = strided[
                group, pl.ds(load, steps, stride=loads), :
            ]


def write_chunks(ints, base, by_load, outs, share, steps):
    for index, out in enumerate(outs):
        first = ints[base + index]
        for item in range(share):
            out[item * steps : (item + 1) * steps] = by_load[first + item]


def far_first_kernel(
    slots, span, couplings, share, ints, past, kernels, *refs
):
    (*outs, kernel_buffer, total, strided, by_load, sems) = refs
    steps = past.shape[0] - span
    loads, columns = past.shape[1:]
    rows = total.shape[1]
    start_slots(ints, kernels, kernel_buffer, sems)

    def window_of(start):
        return past[pl.ds(start, steps)].reshape(steps * loads, columns)

    sum_slots(ints, window_of, kernels, kernel_buffer, sems, total, span)
    split_loads(total, strided, by_load, loads, steps)
    base = 1 + slots
    write_chunks(ints, base, by_load, outs, share, steps)
    holds = ints[base + len(outs)] > 0
    at = pl.multiple_of(ints[base + len(outs) + 1] * rows, LANES)
    recent = past[past.shape[0] - couplings :, :, pl.ds(at, rows)].astype(F32)
    recent = jnp.where(holds, recent, jnp.zeros_like(recent))
    for step in range(couplings):
        for group in range(rows // LANES):
            strided[group, step * loads : (step + 1) * loads] = recent[
                step, :, group * LANES : (group + 1) * LANES
            ]
    for index, out in enumerate(outs):
        first = ints[base + index]
        out[share * steps :] = jnp.zeros_like(out[share * steps :])
        for item in range(share):
            for step in range(couplings):
                row = share * steps + item * couplings + step
                for group in range(rows // LANES):
                    out[row : row + 1, group * LANES : (group + 1) * LANES] = strided[
                        group, pl.ds(step * loads + first + item, 1), :
                    ]


def far_next_kernel(slots, span, share, ratio, ints, past, kernels, *refs):
    chunk_count = len(refs) - 8
    half = chunk_count
    (*rest, kernel_buffer, total, strided, by_load, stage, history, sems, past_sem) = refs
    sources = (len(rest)) // 2
    chunks, outs = rest[:sources], rest[sources:]
    loads, columns = past.shape[1:]
    rows = total.shape[1]
    steps = history.shape[0] - span
    start_slots(ints, kernels, kernel_buffer, sems)
    tail = pltpu.make_async_copy(
        past.at[pl.ds(steps, span)], history.at[pl.ds(0, span)], past_sem
    )
    tail.start()
    base = 1 + slots + len(outs)
    for index, chunk in enumerate(chunks):
        first = ints[base + index]
        for part in range(ratio):
            for item in range(share):
                stage[first + item, :, part * rows : (part + 1) * rows] = chunk[
                    part, item * steps : (item + 1) * steps
                ].astype(F32)
    groups = columns // LANES
    for group in range(groups):
        for load in range(loads):
            strided[group, pl.ds(load, steps, stride=loads), :] = stage[
                load, :, group * LANES : (group + 1) * LANES
            ]
    for group in range(groups):
        history[span:, :, group * LANES : (group + 1) * LANES] = (
            strided[group].reshape(steps, loads, LANES).astype(BF16)
        )
    tail.wait()

    def window_of(start):
        return history[pl.ds(start, steps)].reshape(steps * loads, columns)

    sum_slots(ints, window_of, kernels, kernel_buffer, sems, total, span)
    split_loads(total, strided.at[pl.ds(0, rows // LANES)], by_load, loads, steps)
    write_chunks(ints, 1 + slots, by_load, outs, share, steps)


def prepare_kernel(levels, couplings, inverse, *refs):
    (
        inverse_high,
        inverse_low,
        coupling_high,
        coupling_low,
        first_high,
        first_low,
        *powers,
        matrix,
    ) = refs
    count, rows, _ = couplings.shape
    high, low = split(inverse[...])
    inverse_high[...] = high
    inverse_low[...] = low
    matrix[...] = jnp.zeros_like(matrix)
    identity = (
        lax.broadcasted_iota(jnp.int32, (rows, rows), 0)
        == lax.broadcasted_iota(jnp.int32, (rows, rows), 1)
    ).astype(F32)
    for lag in range(count):
        coupling_high[lag], coupling_low[lag] = split(couplings[lag])
        matrix[lag * rows : (lag + 1) * rows, :rows] = -dot3(couplings[lag], high, low)
        if lag + 1 < count:
            matrix[
                lag * rows : (lag + 1) * rows, (lag + 1) * rows : (lag + 2) * rows
            ] = identity
    first_high[...], first_low[...] = split(matrix[:rows, :rows])
    power_high, power_low = split(matrix[...])
    for level in range(1, levels):
        wide = powers[2 * (level - 1)].shape[1]
        product = dot3(matrix[...], power_high[:, :wide], power_low[:, :wide])
        power_high, power_low = split(product)
        powers[2 * (level - 1)][...] = power_high
        powers[2 * (level - 1) + 1][...] = power_low
        if level + 1 < levels:
            matrix[...] = product


def solve_kernel(steps, share, levels, parts, packed, *refs):
    partials, refs = refs[:parts], refs[parts:]
    (
        driving,
        earlier,
        inverse_high,
        inverse_low,
        coupling_high,
        coupling_low,
        first_high,
        first_low,
        *powers,
    ) = refs[: 8 + 2 * (levels - 1)]
    solved, rounded, state = refs[8 + 2 * (levels - 1) :]
    count, rows, _ = coupling_high.shape
    size = share * steps
    far = partials[0][...]
    for partial in partials[1:]:
        far = far + partial[...]
    adjusted = driving[...].astype(F32) - far[:size]
    row_of = lax.broadcasted_iota(jnp.int32, (size, 1), 0)
    padded = -(-share // SUBLANES) * SUBLANES
    known = far[size:] if packed else earlier[...]

    def back(lag):
        pieces = [
            known[item * count + count - lag : item * count + count - lag + 1]
            for item in range(share)
        ]
        pieces.append(jnp.zeros((padded - share, rows), F32))
        return jnp.concatenate(pieces, 0)

    for step in range(count):
        pull = None
        for lag in range(step + 1, count + 1):
            term = dot3(back(lag - step), coupling_high[lag - 1], coupling_low[lag - 1])
            pull = term if pull is None else pull + term
        for item in range(share):
            adjusted = adjusted - jnp.where(
                row_of == item * steps + step, pull[item : item + 1], 0.0
            )
    within = row_of % steps
    driven = dot3(adjusted, inverse_high[...], inverse_low[...])

    def delayed(value, delay):
        return jnp.where(within >= delay, pltpu.roll(value, delay, 0), 0.0)

    columns = [driven + delayed(dot3(driven, first_high[...], first_low[...]), 1)]
    if count > 1:
        columns.append(delayed(driven, 1))
    columns += [jnp.zeros_like(driven)] * (count - 2)
    total = jnp.concatenate(columns, 1)
    for level in range(1, levels):
        high, low = powers[2 * (level - 1)], powers[2 * (level - 1) + 1]
        wide = high.shape[1]
        total = total[:, :wide] + delayed(dot3(total, high[...], low[...]), 2**level)
    result = total[:, :rows]
    solved[...] = result
    rounded[...] = result.astype(BF16)
    state[...] = jnp.zeros_like(state)
    for item in range(share):
        state[item * count : (item + 1) * count] = result[
            (item + 1) * steps - count : (item + 1) * steps
        ]


def spread_kernel(steps, share, ints, *refs):
    (*chunks, out, by_load, strided) = refs
    loads, rows = out.shape[1:]
    for index, chunk in enumerate(chunks):
        first = ints[index]
        for item in range(share):
            by_load[first + item] = chunk[item * steps : (item + 1) * steps]
    for group in range(rows // LANES):
        for load in range(loads):
            strided[group, pl.ds(load, steps, stride=loads), :] = by_load[
                load, :, group * LANES : (group + 1) * LANES
            ]
    for group in range(rows // LANES):
        out[:, :, group * LANES : (group + 1) * LANES] = strided[group].reshape(
            steps, loads, LANES
        )


def landing(plane, sources):
    shares = sorted(range(sources), key=lambda z: (-abs(z - plane), z))
    if sources & (sources - 1) == 0:
        chips = sorted(range(sources), key=lambda e: (bin(e ^ plane).count("1"), e))
    else:
        chips = sorted(range(sources), key=lambda e: (abs(e - plane), e))
    where = [0] * sources
    for one, chip in zip(shares, chips):
        where[one] = chip
    return where


def local(incident, past_density, kernels, lag_offset, lag_counts, couplings, inverse):
    all_steps, loads, rows = incident.shape
    columns = past_density.shape[2]
    slots = kernels.shape[0]
    span = lag_offset.shape[2]
    steps = past_density.shape[0] - span
    blocks = all_steps // steps
    count = couplings.shape[0]
    levels = steps.bit_length() - 1
    ratio = columns // rows
    sources = lax.axis_size("src")
    targets = lax.axis_size("tgt")
    target = lax.axis_index("tgt")
    source = lax.axis_index("src")
    share = max(loads // sources, 1)
    size = share * steps
    groups = rows // LANES
    pad = -(-share * count // SUBLANES) * SUBLANES

    def first_load(member):
        return member * share % loads

    peers = [partner(source, k, sources) for k in range(sources)]
    owners = [sender(source, k, sources) for k in range(sources)]
    wanted = [first_load(member) for member in peers]
    offsets = lag_offset[0, 0, :slots]
    scalars = [lag_counts[0, 0]] + [offsets[slot] for slot in range(slots)]
    holds = (source == target // ratio).astype(jnp.int32)
    ints = jnp.stack(scalars + wanted + [holds, target % ratio]).astype(jnp.int32)

    table = [landing(plane, sources) for plane in range(sources)]
    inverse_table = [
        [table[plane].index(chip) for chip in range(sources)] for plane in range(sources)
    ]
    chip = target // ratio
    back_table = jnp.array(inverse_table, jnp.int32)
    arrived = [
        first_load(back_table[source, sender(chip, k, sources)]) for k in range(sources)
    ]
    ints_next = jnp.stack(scalars + wanted + arrived).astype(jnp.int32)
    ints_spread = jnp.stack([first_load(member) for member in owners]).astype(jnp.int32)

    vector = functools.partial(pltpu.CompilerParams, vmem_limit_bytes=32 * 1024 * 1024)
    far_scratch = [
        pltpu.VMEM(kernels.shape, BF16),
        pltpu.VMEM((steps * loads, rows), F32),
    ]

    def trade(value, axis_shift):
        pairs = [(i, partner(i, axis_shift, sources)) for i in range(sources)]
        return lax.ppermute(value, "src", pairs)

    prepared = pl.pallas_call(
        functools.partial(prepare_kernel, levels),
        out_shape=[jax.ShapeDtypeStruct((rows, rows), BF16)] * 2
        + [jax.ShapeDtypeStruct((count, rows, rows), BF16)] * 2
        + [jax.ShapeDtypeStruct((rows, rows), BF16)] * 2
        + [jax.ShapeDtypeStruct((count * rows, count * rows), BF16)] * (2 * (levels - 2))
        + [jax.ShapeDtypeStruct((count * rows, rows), BF16)] * 2,
        in_specs=[VMEM, VMEM],
        out_specs=[VMEM] * (6 + 2 * (levels - 1)),
        scratch_shapes=[pltpu.VMEM((count * rows, count * rows), F32)],
        compiler_params=vector(),
        cost_estimate=pl.CostEstimate(
            flops=6 * levels * (count * rows) ** 3, bytes_accessed=8 * 2**20, transcendentals=0
        ),
        name="prepare",
    )(couplings, inverse)

    def solve(partials, driving, earlier, packed):
        operands = [*partials, driving, earlier, *prepared]
        return pl.pallas_call(
            functools.partial(solve_kernel, steps, share, levels, len(partials), packed),
            out_shape=[
                jax.ShapeDtypeStruct((size, rows), F32),
                jax.ShapeDtypeStruct((size, rows), BF16),
                jax.ShapeDtypeStruct((pad, rows), F32),
            ],
            in_specs=[VMEM] * len(operands),
            out_specs=[VMEM] * 3,
            compiler_params=vector(),
            name="solve",
        )(*operands)

    def spread(chunks):
        return pl.pallas_call(
            functools.partial(spread_kernel, steps, share),
            out_shape=jax.ShapeDtypeStruct((steps, loads, rows), F32),
            in_specs=[SMEM] + [VMEM] * sources,
            out_specs=VMEM,
            scratch_shapes=[
                pltpu.VMEM((loads, steps, rows), F32),
                pltpu.VMEM((groups, steps * loads, LANES), F32),
            ],
            compiler_params=vector(),
            name="spread",
        )(ints_spread, *chunks)

    own_incident = lax.dynamic_slice_in_dim(incident, first_load(source), share, 1)
    own_incident = own_incident.reshape(blocks, steps, share, rows)
    own_incident = own_incident.transpose(0, 2, 1, 3).reshape(blocks, size, rows)

    partials = pl.pallas_call(
        functools.partial(far_first_kernel, slots, span, count, share),
        out_shape=[jax.ShapeDtypeStruct((size + pad, rows), F32)] * sources,
        in_specs=[SMEM, VMEM, ANY],
        out_specs=[VMEM] * sources,
        scratch_shapes=far_scratch
        + [
            pltpu.VMEM((groups, steps * loads, LANES), F32),
            pltpu.VMEM((loads, steps, rows), F32),
            pltpu.SemaphoreType.DMA((slots,)),
        ],
        compiler_params=vector(),
        name="far_first",
    )(ints, past_density, kernels)

    state = jnp.zeros((pad, rows), F32)
    produced = []
    for block in range(blocks):
        if block > 0:
            moves = [
                (
                    (one * ratio + part) * sources + z,
                    (table[one][z] * ratio + part) * sources + one,
                )
                for one in range(sources)
                for part in range(ratio)
                for z in range(sources)
            ]
            landed = lax.ppermute(rounded, ("tgt", "src"), moves)
            around = [landed]
            for k in range(1, sources):
                pairs = [
                    (e * ratio + part, partner(e, k, sources) * ratio + part)
                    for e in range(sources)
                    for part in range(ratio)
                ]
                around.append(lax.ppermute(landed, "tgt", pairs))
            held = jnp.stack(around)
            parts = [held]
            for turn in range(1, ratio):
                pairs = [
                    (e * ratio + part, e * ratio + (part + turn) % ratio)
                    for e in range(sources)
                    for part in range(ratio)
                ]
                parts.append(lax.ppermute(held, "tgt", pairs))
            every = jnp.stack(parts, 1)
            order = (target % ratio - jnp.arange(ratio)) % ratio
            every = every[:, order]
            partials = pl.pallas_call(
                functools.partial(far_next_kernel, slots, span, share, ratio),
                out_shape=[jax.ShapeDtypeStruct((size, rows), F32)] * sources,
                in_specs=[SMEM, ANY, ANY] + [VMEM] * sources,
                out_specs=[VMEM] * sources,
                scratch_shapes=far_scratch
                + [
                    pltpu.VMEM((columns // LANES, steps * loads, LANES), F32),
                    pltpu.VMEM((loads, steps, rows), F32),
                    pltpu.VMEM((loads, steps, columns), F32),
                    pltpu.VMEM((span + steps, loads, columns), BF16),
                    pltpu.SemaphoreType.DMA((slots,)),
                    pltpu.SemaphoreType.DMA,
                ],
                compiler_params=vector(),
                name="far_next",
            )(ints_next, past_density, kernels, *[every[k] for k in range(sources)])
        received = [partials[0]] + [trade(partials[k], k) for k in range(1, sources)]
        solved, rounded, state = solve(received, own_incident[block], state, block == 0)
        chunks = [solved] + [trade(solved, k) for k in range(1, sources)]
        produced.append(spread(chunks))
    return jnp.concatenate(produced, 0)


def solution(mesh):
    return jax.shard_map(
        local,
        mesh=mesh,
        in_specs=(
            P(None, None, "tgt"),
            P(None, None, "src"),
            P(None, "src", "tgt"),
            P("tgt", "src", None),
            P("tgt", "src"),
            P(None, "tgt", None),
            P("tgt", None),
        ),
        out_specs=P(None, None, "tgt"),
        check_vma=False,
    )
```

```python
import functools

import jax
import jax.numpy as jnp
from jax import lax
from jax.experimental import pallas as pl
from jax.experimental.pallas import tpu as pltpu
from jax.sharding import PartitionSpec as P

F32 = jnp.float32
BF16 = jnp.bfloat16
LANES = 128
SUBLANES = 8
VMEM = pl.BlockSpec(memory_space=pltpu.VMEM)
SMEM = pl.BlockSpec(memory_space=pltpu.SMEM)
HBM = pl.BlockSpec(memory_space=pltpu.HBM)


def partner(index, shift, count):
    if count & (count - 1) == 0:
        return index ^ shift
    return (index + shift) % count


def sender(index, shift, count):
    if count & (count - 1) == 0:
        return index ^ shift
    return (index - shift) % count


def split(value):
    high = value.astype(BF16)
    return high, (value - high.astype(F32)).astype(BF16)


def dot3(value, high, low):
    rows = value.shape[0]
    value_high, value_low = split(value)
    both = jnp.dot(
        jnp.concatenate([value_high, value_low], 0), high, preferred_element_type=F32
    )
    cross = jnp.dot(value_high, low, preferred_element_type=F32)
    return both[:rows] + (both[rows:] + cross)


HEADROOM = 13.0
SMALLEST = 2.0**-100


def scaled(chunk):
    largest = jnp.max(jnp.max(jnp.abs(chunk), axis=0, keepdims=True), axis=1, keepdims=True)
    power = jnp.floor(jnp.log2(jnp.maximum(largest, SMALLEST)))
    return chunk * jnp.exp2(HEADROOM - power), power


def unscaled(packed, size, row):
    return packed[:size] * jnp.exp2(packed[row : row + 1] - HEADROOM)


def start_slots(counts, kernels, kernel_buffer, sems):
    for slot in range(kernel_buffer.shape[0]):

        @pl.when(slot < counts[0, 0])
        def _():
            pltpu.make_async_copy(
                kernels.at[slot], kernel_buffer.at[slot], sems.at[slot]
            ).start()


def sum_slots(counts, offsets, history, kernels, kernel_buffer, sems, total, span):
    steps = history.shape[0] - span
    loads, columns = history.shape[1:]
    total[...] = jnp.zeros_like(total)

    def add(slot, carry):
        pltpu.make_async_copy(
            kernels.at[slot], kernel_buffer.at[slot], sems.at[slot]
        ).wait()
        window = history[pl.ds(span - offsets[0, 0, slot], steps)]
        total[...] += jnp.dot(
            window.reshape(steps * loads, columns),
            kernel_buffer[slot],
            preferred_element_type=F32,
        )
        return carry

    lax.fori_loop(0, counts[0, 0], add, 0)


def split_loads(total, strided, by_load, loads, steps):
    for group in range(total.shape[1] // LANES):
        lanes = slice(group * LANES, (group + 1) * LANES)
        strided[group] = total[:, lanes]
        for load in range(loads):
            by_load[load, :, lanes] = strided[group, pl.ds(load, steps, stride=loads), :]


def write_chunks(by_load, outs, share, row, sources):
    loads, steps, rows = by_load.shape
    size = share * steps
    source = lax.axis_index("src")
    for index, out in enumerate(outs):
        first = partner(source, index, sources) * share % loads
        for item in range(share):
            out[item * steps : (item + 1) * steps] = by_load[first + item]
        if index > 0:
            out[:size], power = scaled(out[:size])
            out[row : row + 1] = jnp.broadcast_to(power, (1, rows))
        else:
            out[row : row + 1] = jnp.full((1, rows), HEADROOM, F32)


def far_first_kernel(
    span, couplings, share, sources, ratio, counts, offsets, past, kernels, *refs
):
    (*outs, history, kernel_buffer, total, strided, by_load, sems, past_sem) = refs
    fetched = pltpu.make_async_copy(past, history, past_sem)
    fetched.start()
    start_slots(counts, kernels, kernel_buffer, sems)
    steps = history.shape[0] - span
    loads = history.shape[1]
    rows = total.shape[1]
    size = share * steps
    fetched.wait()
    sum_slots(counts, offsets, history, kernels, kernel_buffer, sems, total, span)
    split_loads(total, strided, by_load, loads, steps)
    target, source = lax.axis_index("tgt"), lax.axis_index("src")
    holds = source == target // ratio
    at = pl.multiple_of(target % ratio * rows, LANES)
    recent = history[history.shape[0] - couplings :, :, pl.ds(at, rows)].astype(F32)
    recent = jnp.where(holds, recent, jnp.zeros_like(recent))
    for step in range(couplings):
        for group in range(rows // LANES):
            strided[group, step * loads : (step + 1) * loads] = recent[
                step, :, group * LANES : (group + 1) * LANES
            ]
    for index, out in enumerate(outs):
        first = partner(source, index, sources) * share % loads
        out[size:] = jnp.zeros_like(out[size:])
        for item in range(share):
            for step in range(couplings):
                row = size + item * couplings + step
                for group in range(rows // LANES):
                    out[row : row + 1, group * LANES : (group + 1) * LANES] = strided[
                        group, pl.ds(step * loads + first + item, 1), :
                    ]
    write_chunks(by_load, outs, share, size + share * couplings, sources)


def far_next_kernel(
    span, couplings, share, sources, ratio, counts, offsets, firsts, past, kernels, *refs
):
    arrived, refs = refs[: sources * ratio], refs[sources * ratio :]
    (*outs, kernel_buffer, total, strided, by_load, stage, history, sems, past_sem) = refs
    steps = history.shape[0] - span
    loads, columns = history.shape[1:]
    rows = total.shape[1]
    start_slots(counts, kernels, kernel_buffer, sems)
    tail = pltpu.make_async_copy(
        past.at[pl.ds(steps, span)], history.at[pl.ds(0, span)], past_sem
    )
    tail.start()
    own = lax.axis_index("tgt") % ratio
    for index in range(sources):
        first = firsts[0, 0, index]
        for turn in range(ratio):
            chunk = arrived[turn * sources + index]
            part = lax.rem(own + ratio - turn, ratio)
            for item in range(share):
                stage[part, first + item] = chunk[
                    item * steps : (item + 1) * steps
                ].astype(F32)
    for group in range(columns // LANES):
        part, at = divmod(group * LANES, rows)
        for load in range(loads):
            strided[group, pl.ds(load, steps, stride=loads), :] = stage[
                part, load, :, at : at + LANES
            ]
        history[span:, :, group * LANES : (group + 1) * LANES] = (
            strided[group].reshape(steps, loads, LANES).astype(BF16)
        )
    tail.wait()
    sum_slots(counts, offsets, history, kernels, kernel_buffer, sems, total, span)
    split_loads(total, strided, by_load, loads, steps)
    write_chunks(by_load, outs, share, share * steps, sources)


def prepare_kernel(levels, couplings, inverse, *refs):
    (
        inverse_high,
        inverse_low,
        coupling_high,
        coupling_low,
        first_high,
        first_low,
        *powers,
        matrix,
    ) = refs
    count, rows, _ = couplings.shape
    high, low = split(inverse[...])
    inverse_high[...] = high
    inverse_low[...] = low
    matrix[...] = jnp.zeros_like(matrix)
    identity = (
        lax.broadcasted_iota(jnp.int32, (rows, rows), 0)
        == lax.broadcasted_iota(jnp.int32, (rows, rows), 1)
    ).astype(F32)
    for lag in range(count):
        coupling_high[lag], coupling_low[lag] = split(couplings[lag])
        matrix[lag * rows : (lag + 1) * rows, :rows] = -dot3(couplings[lag], high, low)
        if lag + 1 < count:
            matrix[
                lag * rows : (lag + 1) * rows, (lag + 1) * rows : (lag + 2) * rows
            ] = identity
    first_high[...], first_low[...] = split(matrix[:rows, :rows])
    power_high, power_low = split(matrix[...])
    for level in range(1, levels):
        wide = powers[2 * (level - 1)].shape[1]
        product = dot3(matrix[...], power_high[:, :wide], power_low[:, :wide])
        power_high, power_low = split(product)
        powers[2 * (level - 1)][...] = power_high
        powers[2 * (level - 1) + 1][...] = power_low
        if level + 1 < levels:
            matrix[...] = product


def solve_kernel(steps, share, levels, parts, packed, *refs):
    partials, refs = refs[:parts], refs[parts:]
    (
        driving,
        earlier,
        inverse_high,
        inverse_low,
        coupling_high,
        coupling_low,
        first_high,
        first_low,
        *powers,
    ) = refs[: 8 + 2 * (levels - 1)]
    solved, rounded, state, sent = refs[8 + 2 * (levels - 1) :]
    count, rows, _ = coupling_high.shape
    size = share * steps
    power_row = size + share * count if packed else size
    adjusted = driving[...].astype(F32)
    for partial in partials:
        adjusted = adjusted - unscaled(partial, size, power_row)
    row_of = lax.broadcasted_iota(jnp.int32, (size, 1), 0)
    padded = -(-share // SUBLANES) * SUBLANES
    if packed:
        known = partials[0][size:]
        for partial in partials[1:]:
            known = known + partial[size:]
    else:
        known = earlier[...]

    def back(lag):
        pieces = [
            known[item * count + count - lag : item * count + count - lag + 1]
            for item in range(share)
        ]
        pieces.append(jnp.zeros((padded - share, rows), F32))
        return jnp.concatenate(pieces, 0)

    for step in range(count):
        pull = None
        for lag in range(step + 1, count + 1):
            term = dot3(back(lag - step), coupling_high[lag - 1], coupling_low[lag - 1])
            pull = term if pull is None else pull + term
        for item in range(share):
            adjusted = adjusted - jnp.where(
                row_of == item * steps + step, pull[item : item + 1], 0.0
            )
    within = row_of % steps
    driven = dot3(adjusted, inverse_high[...], inverse_low[...])

    def delayed(value, delay):
        return jnp.where(within >= delay, pltpu.roll(value, delay, 0), 0.0)

    columns = [driven + delayed(dot3(driven, first_high[...], first_low[...]), 1)]
    if count > 1:
        columns.append(delayed(driven, 1))
    columns += [jnp.zeros_like(driven)] * (count - 2)
    total = jnp.concatenate(columns, 1)
    for level in range(1, levels):
        high, low = powers[2 * (level - 1)], powers[2 * (level - 1) + 1]
        wide = high.shape[1]
        total = total[:, :wide] + delayed(dot3(total, high[...], low[...]), 2**level)
    result = total[:, :rows]
    solved[...] = result
    rounded[...] = result.astype(BF16)
    sent[:size], power = scaled(result)
    sent[size:] = jnp.broadcast_to(power, (sent.shape[0] - size, rows))
    state[...] = jnp.zeros_like(state)
    for item in range(share):
        state[item * count : (item + 1) * count] = result[
            (item + 1) * steps - count : (item + 1) * steps
        ]


def spread_kernel(steps, share, own, *refs):
    (*chunks, out, by_load, strided) = refs
    loads, rows = out.shape[1:]
    sources = len(chunks) + 1
    size = share * steps
    source = lax.axis_index("src")
    for index, chunk in enumerate([own, *chunks]):
        first = sender(source, index, sources) * share % loads
        value = chunk[...] if index == 0 else unscaled(chunk, size, size)
        for item in range(share):
            by_load[first + item] = value[item * steps : (item + 1) * steps]
    for group in range(rows // LANES):
        lanes = slice(group * LANES, (group + 1) * LANES)
        for load in range(loads):
            strided[group, pl.ds(load, steps, stride=loads), :] = by_load[load, :, lanes]
        out[:, :, lanes] = strided[group].reshape(steps, loads, LANES)


def landing(plane, sources):
    shares = sorted(range(sources), key=lambda z: (-abs(z - plane), z))
    if sources & (sources - 1) == 0:
        chips = sorted(range(sources), key=lambda e: (bin(e ^ plane).count("1"), e))
    else:
        chips = sorted(range(sources), key=lambda e: (abs(e - plane), e))
    where = [0] * sources
    for one, chip in zip(shares, chips):
        where[one] = chip
    return where


def local(incident, past_density, kernels, lag_offset, lag_counts, couplings, inverse):
    all_steps, loads, rows = incident.shape
    columns = past_density.shape[2]
    slots = kernels.shape[0]
    span = lag_offset.shape[2]
    steps = past_density.shape[0] - span
    blocks = all_steps // steps
    count = couplings.shape[0]
    levels = steps.bit_length() - 1
    ratio = columns // rows
    sources = lax.axis_size("src")
    targets = lax.axis_size("tgt")
    target = lax.axis_index("tgt")
    source = lax.axis_index("src")
    share = max(loads // sources, 1)
    size = share * steps
    groups = rows // LANES
    pad = -(-(share * count + 1) // SUBLANES) * SUBLANES

    table = [landing(plane, sources) for plane in range(sources)]
    firsts = [
        [
            [
                table[plane].index(sender(chip, k, sources)) * share % loads
                for k in range(sources)
            ]
            for plane in range(sources)
        ]
        for chip in range(sources)
    ]
    firsts = lax.dynamic_slice(
        jnp.array(firsts, jnp.int32), (target // ratio, source, 0), (1, 1, sources)
    )

    def params(mebibytes):
        return pltpu.CompilerParams(vmem_limit_bytes=mebibytes * 2**20)

    def cost(work):
        return pl.CostEstimate(flops=work * 10**9, bytes_accessed=0, transcendentals=0)

    def trade(value, shift):
        pairs = [(i, partner(i, shift, sources)) for i in range(sources)]
        return lax.ppermute(value, "src", pairs)

    def trade_each(values):
        return [
            trade(value.astype(jnp.float16), k).astype(F32)
            for k, value in enumerate(values, 1)
        ]

    prepared = pl.pallas_call(
        functools.partial(prepare_kernel, levels),
        out_shape=[jax.ShapeDtypeStruct((rows, rows), BF16)] * 2
        + [jax.ShapeDtypeStruct((count, rows, rows), BF16)] * 2
        + [jax.ShapeDtypeStruct((rows, rows), BF16)] * 2
        + [jax.ShapeDtypeStruct((count * rows, count * rows), BF16)] * (2 * (levels - 2))
        + [jax.ShapeDtypeStruct((count * rows, rows), BF16)] * 2,
        in_specs=[VMEM, VMEM],
        out_specs=[VMEM] * (6 + 2 * (levels - 1)),
        scratch_shapes=[pltpu.VMEM((count * rows, count * rows), F32)],
        compiler_params=params(16),
        cost_estimate=cost(5),
        name="prepare",
    )(couplings, inverse)

    def solve(partials, driving, earlier, packed):
        operands = [*partials, driving, earlier, *prepared]
        return pl.pallas_call(
            functools.partial(solve_kernel, steps, share, levels, len(partials), packed),
            out_shape=[
                jax.ShapeDtypeStruct((size, rows), F32),
                jax.ShapeDtypeStruct((size, rows), BF16),
                jax.ShapeDtypeStruct((pad, rows), F32),
                jax.ShapeDtypeStruct((size + SUBLANES, rows), F32),
            ],
            in_specs=[VMEM] * len(operands),
            out_specs=[VMEM] * 4,
            compiler_params=params(12),
            cost_estimate=cost(3),
            name="solve",
        )(*operands)

    def spread(own, chunks):
        return pl.pallas_call(
            functools.partial(spread_kernel, steps, share),
            out_shape=jax.ShapeDtypeStruct((steps, loads, rows), F32),
            in_specs=[VMEM] * sources,
            out_specs=VMEM,
            scratch_shapes=[
                pltpu.VMEM((loads, steps, rows), F32),
                pltpu.VMEM((groups, steps * loads, LANES), F32),
            ],
            compiler_params=params(8),
            name="spread",
        )(own, *chunks)

    own_incident = lax.dynamic_slice_in_dim(incident, source * share % loads, share, 1)
    own_incident = own_incident.reshape(blocks, steps, share, rows)
    own_incident = own_incident.transpose(0, 2, 1, 3).reshape(blocks, size, rows)

    far_scratch = [
        pltpu.VMEM(kernels.shape, BF16),
        pltpu.VMEM((steps * loads, rows), F32),
        pltpu.VMEM((columns // LANES, steps * loads, LANES), F32),
        pltpu.VMEM((loads, steps, rows), F32),
    ]
    far_sems = [pltpu.SemaphoreType.DMA((slots,)), pltpu.SemaphoreType.DMA]
    history_scratch = pltpu.VMEM((span + steps, loads, columns), BF16)

    partials = pl.pallas_call(
        functools.partial(far_first_kernel, span, count, share, sources, ratio),
        out_shape=[jax.ShapeDtypeStruct((size + pad, rows), F32)] * sources,
        in_specs=[SMEM, SMEM, HBM, HBM],
        out_specs=[VMEM] * sources,
        scratch_shapes=[history_scratch, *far_scratch, *far_sems],
        compiler_params=params(12),
        cost_estimate=cost(2),
        name="far_first",
    )(lag_counts, lag_offset, past_density, kernels)

    state = jnp.zeros((pad, rows), F32)
    produced = []
    for block in range(blocks):
        if block > 0:
            moves = [
                (
                    (one * ratio + part) * sources + z,
                    (table[one][z] * ratio + part) * sources + one,
                )
                for one in range(sources)
                for part in range(ratio)
                for z in range(sources)
            ]
            landed = lax.ppermute(rounded, ("tgt", "src"), moves)
            chunks = trade_each([sent] * (sources - 1))
            arrived = [landed]
            for k in range(1, sources):
                pairs = [
                    (e * ratio + part, partner(e, k, sources) * ratio + part)
                    for e in range(sources)
                    for part in range(ratio)
                ]
                arrived.append(lax.ppermute(landed, "tgt", pairs))
            swapped = []
            for turn in range(1, ratio):
                pairs = [
                    (e * ratio + part, e * ratio + (part + turn) % ratio)
                    for e in range(sources)
                    for part in range(ratio)
                ]
                swapped += [lax.ppermute(chunk, "tgt", pairs) for chunk in arrived]
            partials = pl.pallas_call(
                functools.partial(far_next_kernel, span, count, share, sources, ratio),
                out_shape=[jax.ShapeDtypeStruct((size + SUBLANES, rows), F32)] * sources,
                in_specs=[SMEM, SMEM, SMEM, HBM, HBM] + [VMEM] * (sources * ratio),
                out_specs=[VMEM] * sources,
                scratch_shapes=far_scratch
                + [pltpu.VMEM((ratio, loads, steps, rows), F32), history_scratch]
                + far_sems,
                compiler_params=params(12),
                cost_estimate=cost(3),
                name="far_next",
            )(lag_counts, lag_offset, firsts, past_density, kernels, *arrived, *swapped)
            produced.append(spread(solved, chunks))
        received = [partials[0]] + trade_each(partials[1:])
        solved, rounded, state, sent = solve(
            received, own_incident[block], state, block == 0
        )
    produced.append(spread(solved, trade_each([sent] * (sources - 1))))
    return jnp.concatenate(produced, 0)


def solution(mesh):
    return jax.shard_map(
        local,
        mesh=mesh,
        in_specs=(
            P(None, None, "tgt"),
            P(None, None, "src"),
            P(None, "src", "tgt"),
            P("tgt", "src", None),
            P("tgt", "src"),
            P(None, "tgt", None),
            P("tgt", None),
        ),
        out_specs=P(None, None, "tgt"),
        check_vma=False,
    )
```

```python
import functools

import jax
import jax.numpy as jnp
from jax import lax
from jax.experimental import pallas as pl
from jax.experimental.pallas import tpu as pltpu
from jax.sharding import PartitionSpec as P

F32 = jnp.float32
BF16 = jnp.bfloat16
LANES = 128
SUBLANES = 8
VMEM = pl.BlockSpec(memory_space=pltpu.VMEM)
SMEM = pl.BlockSpec(memory_space=pltpu.SMEM)
HBM = pl.BlockSpec(memory_space=pltpu.HBM)


def partner(index, shift, count):
    if count & (count - 1) == 0:
        return index ^ shift
    return (index + shift) % count


def sender(index, shift, count):
    if count & (count - 1) == 0:
        return index ^ shift
    return (index - shift) % count


def split(value):
    high = value.astype(BF16)
    return high, (value - high.astype(F32)).astype(BF16)


def dot3(value, high, low):
    rows = value.shape[0]
    value_high, value_low = split(value)
    both = jnp.dot(
        jnp.concatenate([value_high, value_low], 0), high, preferred_element_type=F32
    )
    cross = jnp.dot(value_high, low, preferred_element_type=F32)
    return both[:rows] + (both[rows:] + cross)


HEADROOM = 13.0
SMALLEST = 2.0**-100


def scaled(chunk):
    largest = jnp.max(jnp.max(jnp.abs(chunk), axis=0, keepdims=True), axis=1, keepdims=True)
    power = jnp.floor(jnp.log2(jnp.maximum(largest, SMALLEST)))
    return chunk * jnp.exp2(HEADROOM - power), power


def unscaled(packed, size, row):
    return packed[:size] * jnp.exp2(packed[row : row + 1] - HEADROOM)


def start_slots(counts, kernels, kernel_buffer, sems):
    for slot in range(kernel_buffer.shape[0]):

        @pl.when(slot < counts[0, 0])
        def _():
            pltpu.make_async_copy(
                kernels.at[slot], kernel_buffer.at[slot], sems.at[slot]
            ).start()


def sum_slots(counts, offsets, history, kernels, kernel_buffer, sems, total, span):
    steps = history.shape[0] - span
    loads, columns = history.shape[1:]
    count = counts[0, 0]
    total[...] = jnp.zeros_like(total)

    def window(slot):
        taken = history[pl.ds(span - offsets[0, 0, slot], steps)]
        return taken.reshape(steps * loads, columns)

    def add(first, together):
        for slot in range(together):
            pltpu.make_async_copy(
                kernels.at[first + slot], kernel_buffer.at[first + slot], sems.at[first + slot]
            ).wait()
        windows = jnp.concatenate([window(first + slot) for slot in range(together)], 1)
        matrix = kernel_buffer[pl.ds(first, together)].reshape(together * columns, -1)
        product = jnp.dot(windows, matrix, preferred_element_type=F32)
        for group in range(total.shape[0]):
            total[group] += product[:, group * LANES : (group + 1) * LANES]

    done = 0
    together = 1 << (kernel_buffer.shape[0].bit_length() - 1)
    while together:
        rounds = (count - done) // together

        def step(index, carry, first=done, together=together):
            add(first + index * together, together)
            return carry

        lax.fori_loop(0, rounds, step, 0)
        done += rounds * together
        together //= 2


def write_chunks(total, outs, share, loads, row):
    groups, size, _ = total.shape
    steps = size // loads
    source, sources = lax.axis_index("src"), len(outs)
    for index, out in enumerate(outs):
        first = partner(source, index, sources) * share % loads
        columns = [
            jnp.concatenate(
                [
                    total[group, pl.ds(first + item, steps, stride=loads), :]
                    for item in range(share)
                ],
                0,
            )
            for group in range(groups)
        ]
        chunk = jnp.concatenate(columns, 1)
        if index > 0:
            chunk, power = scaled(chunk)
        else:
            power = jnp.full((1, 1), HEADROOM, F32)
        out[: share * steps] = chunk
        out[row : row + 1] = jnp.broadcast_to(power, (1, groups * LANES))


def far_first_kernel(
    span, couplings, share, sources, ratio, counts, offsets, past, kernels, *refs
):
    (*outs, tail, history, kernel_buffer, total, sems, past_sem) = refs
    fetched = pltpu.make_async_copy(past, history, past_sem)
    fetched.start()
    start_slots(counts, kernels, kernel_buffer, sems)
    steps = history.shape[0] - span
    loads = history.shape[1]
    groups = total.shape[0]
    rows = groups * LANES
    size = share * steps
    fetched.wait()
    tail[...] = history[steps:]
    sum_slots(counts, offsets, history, kernels, kernel_buffer, sems, total, span)
    for out in outs:
        out[size:] = jnp.zeros_like(out[size:])
    write_chunks(total, outs, share, loads, size + share * couplings)
    target, source = lax.axis_index("tgt"), lax.axis_index("src")
    holds = source == target // ratio
    at = pl.multiple_of(target % ratio * rows, LANES)
    recent = history[history.shape[0] - couplings :, :, pl.ds(at, rows)].astype(F32)
    recent = jnp.where(holds, recent, jnp.zeros_like(recent)).reshape(couplings * loads, rows)
    for group in range(groups):
        total[group, : couplings * loads] = recent[:, group * LANES : (group + 1) * LANES]
    for index, out in enumerate(outs):
        first = partner(source, index, sources) * share % loads
        for item in range(share):
            for step in range(couplings):
                row = size + item * couplings + step
                for group in range(groups):
                    out[row : row + 1, group * LANES : (group + 1) * LANES] = total[
                        group, pl.ds(step * loads + first + item, 1), :
                    ]


def far_next_kernel(table, span, share, ratio, counts, offsets, tail, kernels, *refs):
    sources = len(table)
    arrived, refs = refs[: sources * ratio], refs[sources * ratio :]
    (*outs, kernel_buffer, total, strided, history, sems) = refs
    steps = history.shape[0] - span
    loads, columns = history.shape[1:]
    groups = total.shape[0]
    start_slots(counts, kernels, kernel_buffer, sems)
    history[:span] = tail[...]
    target, source = lax.axis_index("tgt"), lax.axis_index("src")
    chip, own = target // ratio, lax.rem(target, ratio)
    for index in range(sources):
        first = 0
        for plane in range(sources):
            for one in range(sources):
                here = partner(table[plane][one], index, sources)
                first = jnp.where(
                    (source == plane) & (chip == here), one * share % loads, first
                )
        for turn in range(ratio):
            chunk = arrived[turn * sources + index]
            part = lax.rem(own + ratio - turn, ratio)
            for item in range(share):
                for group in range(groups):
                    strided[
                        part * groups + group,
                        pl.ds(first + item, steps, stride=loads),
                        :,
                    ] = chunk[
                        item * steps : (item + 1) * steps, group * LANES : (group + 1) * LANES
                    ].astype(F32)
    for group in range(columns // LANES):
        history[span:, :, group * LANES : (group + 1) * LANES] = (
            strided[group].reshape(steps, loads, LANES).astype(BF16)
        )
    sum_slots(counts, offsets, history, kernels, kernel_buffer, sems, total, span)
    write_chunks(total, outs, share, loads, share * steps)


def prepare_kernel(levels, couplings, inverse, *refs):
    (
        inverse_high,
        inverse_low,
        coupling_high,
        coupling_low,
        first_high,
        first_low,
        *powers,
        matrix,
    ) = refs
    count, rows, _ = couplings.shape
    high, low = split(inverse[...])
    inverse_high[...] = high
    inverse_low[...] = low
    matrix[...] = jnp.zeros_like(matrix)
    identity = (
        lax.broadcasted_iota(jnp.int32, (rows, rows), 0)
        == lax.broadcasted_iota(jnp.int32, (rows, rows), 1)
    ).astype(F32)
    for lag in range(count):
        coupling_high[lag], coupling_low[lag] = split(couplings[lag])
        matrix[lag * rows : (lag + 1) * rows, :rows] = -dot3(couplings[lag], high, low)
        if lag + 1 < count:
            matrix[
                lag * rows : (lag + 1) * rows, (lag + 1) * rows : (lag + 2) * rows
            ] = identity
    first_high[...], first_low[...] = split(matrix[:rows, :rows])
    power_high, power_low = split(matrix[...])
    for level in range(1, levels):
        wide = powers[2 * (level - 1)].shape[1]
        if level == 1 and wide == count * rows:
            column = matrix[:, :rows]
            product = dot3(column, first_high[...], first_low[...])
            product += jnp.concatenate([column[rows:], jnp.zeros((rows, rows), F32)], 0)
            product = jnp.concatenate([product, matrix[:, : wide - rows]], 1)
        else:
            product = dot3(matrix[...], power_high[:, :wide], power_low[:, :wide])
        power_high, power_low = split(product)
        powers[2 * (level - 1)][...] = power_high
        powers[2 * (level - 1) + 1][...] = power_low
        if level + 1 < levels:
            matrix[...] = product


def solve_kernel(steps, share, levels, parts, packed, *refs):
    partials, refs = refs[:parts], refs[parts:]
    (
        driving,
        earlier,
        inverse_high,
        inverse_low,
        coupling_high,
        coupling_low,
        first_high,
        first_low,
        *powers,
    ) = refs[: 8 + 2 * (levels - 1)]
    solved, rounded, state, sent = refs[8 + 2 * (levels - 1) :]
    count, rows, _ = coupling_high.shape
    size = share * steps
    power_row = size + share * count if packed else size
    adjusted = driving[...].astype(F32)
    for partial in partials:
        adjusted = adjusted - unscaled(partial, size, power_row)
    row_of = lax.broadcasted_iota(jnp.int32, (size, 1), 0)
    padded = -(-share // SUBLANES) * SUBLANES
    if packed:
        known = partials[0][size:]
        for partial in partials[1:]:
            known = known + partial[size:]
    else:
        known = earlier[...]

    def back(lag):
        pieces = [
            known[item * count + count - lag : item * count + count - lag + 1]
            for item in range(share)
        ]
        pieces.append(jnp.zeros((padded - share, rows), F32))
        return jnp.concatenate(pieces, 0)

    for step in range(count):
        pull = None
        for lag in range(step + 1, count + 1):
            term = dot3(back(lag - step), coupling_high[lag - 1], coupling_low[lag - 1])
            pull = term if pull is None else pull + term
        for item in range(share):
            adjusted = adjusted - jnp.where(
                row_of == item * steps + step, pull[item : item + 1], 0.0
            )
    within = row_of % steps
    driven = dot3(adjusted, inverse_high[...], inverse_low[...])

    def delayed(value, delay):
        return jnp.where(within >= delay, pltpu.roll(value, delay, 0), 0.0)

    columns = [driven + delayed(dot3(driven, first_high[...], first_low[...]), 1)]
    if count > 1:
        columns.append(delayed(driven, 1))
    columns += [jnp.zeros_like(driven)] * (count - 2)
    total = jnp.concatenate(columns, 1)
    for level in range(1, levels):
        high, low = powers[2 * (level - 1)], powers[2 * (level - 1) + 1]
        wide = high.shape[1]
        total = total[:, :wide] + delayed(dot3(total, high[...], low[...]), 2**level)
    result = total[:, :rows]
    solved[...] = result
    rounded[...] = result.astype(BF16)
    sent[:size], power = scaled(result)
    sent[size:] = jnp.broadcast_to(power, (sent.shape[0] - size, rows))
    state[...] = jnp.zeros_like(state)
    for item in range(share):
        state[item * count : (item + 1) * count] = result[
            (item + 1) * steps - count : (item + 1) * steps
        ]


def spread_kernel(block, share, own, *refs):
    (*chunks, out, strided, ready, sem) = refs
    steps, loads, rows = ready.shape
    sources = (len(chunks) + 1) if block == 0 else len(chunks)
    size = share * steps
    source = lax.axis_index("src")
    for index, chunk in enumerate([own, *chunks][:sources]):
        first = sender(source, index, sources) * share % loads
        value = chunk[...] if index == 0 else unscaled(chunk, size, size)
        for item in range(share):
            for group in range(rows // LANES):
                strided[group, pl.ds(first + item, steps, stride=loads), :] = value[
                    item * steps : (item + 1) * steps, group * LANES : (group + 1) * LANES
                ]
    for group in range(rows // LANES):
        ready[:, :, group * LANES : (group + 1) * LANES] = strided[group].reshape(
            steps, loads, LANES
        )
    copy = pltpu.make_async_copy(ready, out.at[pl.ds(block * steps, steps)], sem)
    copy.start()
    copy.wait()


def landing(plane, sources):
    shares = sorted(range(sources), key=lambda z: (-abs(z - plane), z))
    if sources & (sources - 1) == 0:
        chips = sorted(range(sources), key=lambda e: (bin(e ^ plane).count("1"), e))
    else:
        chips = sorted(range(sources), key=lambda e: (abs(e - plane), e))
    where = [0] * sources
    for one, chip in zip(shares, chips):
        where[one] = chip
    return where


def local(incident, past_density, kernels, lag_offset, lag_counts, couplings, inverse):
    all_steps, loads, rows = incident.shape
    columns = past_density.shape[2]
    slots = kernels.shape[0]
    span = lag_offset.shape[2]
    steps = past_density.shape[0] - span
    blocks = all_steps // steps
    count = couplings.shape[0]
    levels = steps.bit_length() - 1
    ratio = columns // rows
    sources = lax.axis_size("src")
    targets = lax.axis_size("tgt")
    target = lax.axis_index("tgt")
    source = lax.axis_index("src")
    share = max(loads // sources, 1)
    size = share * steps
    groups = rows // LANES
    pad = -(-(share * count + 1) // SUBLANES) * SUBLANES

    table = [landing(plane, sources) for plane in range(sources)]

    def params(mebibytes):
        return pltpu.CompilerParams(vmem_limit_bytes=mebibytes * 2**20)

    def cost(work):
        return pl.CostEstimate(flops=work * 10**9, bytes_accessed=0, transcendentals=0)

    def trade(value, shift):
        pairs = [(i, partner(i, shift, sources)) for i in range(sources)]
        return lax.ppermute(value, "src", pairs)

    def trade_each(values):
        return [
            trade(value.astype(jnp.float16), k).astype(F32)
            for k, value in enumerate(values, 1)
        ]

    prepared = pl.pallas_call(
        functools.partial(prepare_kernel, levels),
        out_shape=[jax.ShapeDtypeStruct((rows, rows), BF16)] * 2
        + [jax.ShapeDtypeStruct((count, rows, rows), BF16)] * 2
        + [jax.ShapeDtypeStruct((rows, rows), BF16)] * 2
        + [jax.ShapeDtypeStruct((count * rows, count * rows), BF16)] * (2 * (levels - 2))
        + [jax.ShapeDtypeStruct((count * rows, rows), BF16)] * 2,
        in_specs=[VMEM, VMEM],
        out_specs=[VMEM] * (6 + 2 * (levels - 1)),
        scratch_shapes=[pltpu.VMEM((count * rows, count * rows), F32)],
        compiler_params=params(16),
        cost_estimate=cost(5),
        name="prepare",
    )(couplings, inverse)

    def solve(partials, driving, earlier, packed):
        operands = [*partials, driving, earlier, *prepared]
        return pl.pallas_call(
            functools.partial(solve_kernel, steps, share, levels, len(partials), packed),
            out_shape=[
                jax.ShapeDtypeStruct((size, rows), F32),
                jax.ShapeDtypeStruct((size, rows), BF16),
                jax.ShapeDtypeStruct((pad, rows), F32),
                jax.ShapeDtypeStruct((size + SUBLANES, rows), F32),
            ],
            in_specs=[VMEM] * len(operands),
            out_specs=[VMEM] * 4,
            compiler_params=params(12),
            cost_estimate=cost(3),
            name="solve",
        )(*operands)

    def spread(block, before, own, chunks):
        last = [] if block == 0 else [before]
        return pl.pallas_call(
            functools.partial(spread_kernel, block, share),
            out_shape=jax.ShapeDtypeStruct((all_steps, loads, rows), F32),
            in_specs=[VMEM] * sources + [HBM] * len(last),
            out_specs=HBM,
            scratch_shapes=[
                pltpu.VMEM((groups, steps * loads, LANES), F32),
                pltpu.VMEM((steps, loads, rows), F32),
                pltpu.SemaphoreType.DMA,
            ],
            input_output_aliases={sources: 0} if last else {},
            compiler_params=params(8),
            name="spread",
        )(own, *chunks, *last)

    own_incident = lax.dynamic_slice_in_dim(incident, source * share % loads, share, 1)
    own_incident = own_incident.reshape(blocks, steps, share, rows)
    own_incident = own_incident.transpose(0, 2, 1, 3).reshape(blocks, size, rows)

    far_scratch = [
        pltpu.VMEM(kernels.shape, BF16),
        pltpu.VMEM((groups, steps * loads, LANES), F32),
    ]
    far_sems = pltpu.SemaphoreType.DMA((slots,))
    history_scratch = pltpu.VMEM((span + steps, loads, columns), BF16)

    *partials, tail = pl.pallas_call(
        functools.partial(far_first_kernel, span, count, share, sources, ratio),
        out_shape=[jax.ShapeDtypeStruct((size + pad, rows), F32)] * sources
        + [jax.ShapeDtypeStruct((span, loads, columns), BF16)],
        in_specs=[SMEM, SMEM, HBM, HBM],
        out_specs=[VMEM] * (sources + 1),
        scratch_shapes=[history_scratch, *far_scratch, far_sems, pltpu.SemaphoreType.DMA],
        compiler_params=params(53),
        cost_estimate=cost(2),
        name="far_first",
    )(lag_counts, lag_offset, past_density, kernels)

    state = jnp.zeros((pad, rows), F32)
    output = None
    for block in range(blocks):
        if block > 0:
            moves = [
                (
                    (one * ratio + part) * sources + z,
                    (table[one][z] * ratio + part) * sources + one,
                )
                for one in range(sources)
                for part in range(ratio)
                for z in range(sources)
            ]
            landed = lax.ppermute(rounded, ("tgt", "src"), moves)
            chunks = trade_each([sent] * (sources - 1))
            arrived = [landed]
            for k in range(1, sources):
                pairs = [
                    (e * ratio + part, partner(e, k, sources) * ratio + part)
                    for e in range(sources)
                    for part in range(ratio)
                ]
                arrived.append(lax.ppermute(landed, "tgt", pairs))
            swapped = []
            for turn in range(1, ratio):
                pairs = [
                    (e * ratio + part, e * ratio + (part + turn) % ratio)
                    for e in range(sources)
                    for part in range(ratio)
                ]
                swapped += [lax.ppermute(chunk, "tgt", pairs) for chunk in arrived]
            partials = pl.pallas_call(
                functools.partial(far_next_kernel, table, span, share, ratio),
                out_shape=[jax.ShapeDtypeStruct((size + SUBLANES, rows), F32)] * sources,
                in_specs=[SMEM, SMEM, VMEM, HBM] + [VMEM] * (sources * ratio),
                out_specs=[VMEM] * sources,
                scratch_shapes=far_scratch
                + [
                    pltpu.VMEM((columns // LANES, steps * loads, LANES), F32),
                    history_scratch,
                    far_sems,
                ],
                compiler_params=params(12),
                cost_estimate=cost(3),
                name="far_next",
            )(lag_counts, lag_offset, tail, kernels, *arrived, *swapped)
            output = spread(block - 1, output, solved, chunks)
        received = [partials[0]] + trade_each(partials[1:])
        solved, rounded, state, sent = solve(
            received, own_incident[block], state, block == 0
        )
    return spread(blocks - 1, output, solved, trade_each([sent] * (sources - 1)))


def solution(mesh):
    return jax.shard_map(
        local,
        mesh=mesh,
        in_specs=(
            P(None, None, "tgt"),
            P(None, None, "src"),
            P(None, "src", "tgt"),
            P("tgt", "src", None),
            P("tgt", "src"),
            P(None, "tgt", None),
            P("tgt", None),
        ),
        out_specs=P(None, None, "tgt"),
        check_vma=False,
    )
```

```python
import functools

import jax
import jax.numpy as jnp
from jax import lax
from jax.experimental import pallas as pl
from jax.experimental.pallas import tpu as pltpu
from jax.sharding import PartitionSpec as P

F32 = jnp.float32
BF16 = jnp.bfloat16
LANES = 128
SUBLANES = 8
VMEM = pl.BlockSpec(memory_space=pltpu.VMEM)
SMEM = pl.BlockSpec(memory_space=pltpu.SMEM)
HBM = pl.BlockSpec(memory_space=pltpu.HBM)


def partner(index, shift, count):
    if count & (count - 1) == 0:
        return index ^ shift
    return (index + shift) % count


def sender(index, shift, count):
    if count & (count - 1) == 0:
        return index ^ shift
    return (index - shift) % count


def split(value):
    high = value.astype(BF16)
    return high, (value - high.astype(F32)).astype(BF16)


def dot3(value, high, low):
    rows = value.shape[0]
    value_high, value_low = split(value)
    both = jnp.dot(
        jnp.concatenate([value_high, value_low], 0), high, preferred_element_type=F32
    )
    cross = jnp.dot(value_high, low, preferred_element_type=F32)
    return both[:rows] + (both[rows:] + cross)


HEADROOM = 13.0
SMALLEST = 2.0**-100


def scaled(chunk):
    largest = jnp.max(jnp.max(jnp.abs(chunk), axis=0, keepdims=True), axis=1, keepdims=True)
    power = jnp.floor(jnp.log2(jnp.maximum(largest, SMALLEST)))
    return chunk * jnp.exp2(HEADROOM - power), power


def unscaled(packed, size, row):
    return packed[:size] * jnp.exp2(packed[row : row + 1] - HEADROOM)


def start_slots(counts, kernels, kernel_buffer, sems):
    for slot in range(kernel_buffer.shape[0]):

        @pl.when(slot < counts[0, 0])
        def _():
            pltpu.make_async_copy(
                kernels.at[slot], kernel_buffer.at[slot], sems.at[slot]
            ).start()


def sum_slots(counts, offsets, history, kernels, total, span, arrived=None):
    steps = history.shape[0] - span
    loads, columns = history.shape[1:]
    count = counts[0, 0]
    total[...] = jnp.zeros_like(total)

    def window(slot):
        taken = history[pl.ds(span - offsets[0, 0, slot], steps)]
        return taken.reshape(steps * loads, columns)

    def add(first, together):
        if arrived is not None:
            for slot in range(together):
                arrived(first + slot)
        windows = jnp.concatenate([window(first + slot) for slot in range(together)], 1)
        matrix = kernels[pl.ds(first, together)].reshape(together * columns, -1)
        product = jnp.dot(windows, matrix, preferred_element_type=F32)
        for group in range(total.shape[0]):
            total[group] += product[:, group * LANES : (group + 1) * LANES]

    done = 0
    together = 1 << (kernels.shape[0].bit_length() - 1)
    while together:
        rounds = (count - done) // together

        def step(index, carry, first=done, together=together):
            add(first + index * together, together)
            return carry

        lax.fori_loop(0, rounds, step, 0)
        done += rounds * together
        together //= 2


def write_chunks(total, outs, share, loads, row):
    groups, size, _ = total.shape
    steps = size // loads
    source, sources = lax.axis_index("src"), len(outs)
    for index, out in enumerate(outs):
        first = partner(source, index, sources) * share % loads
        columns = [
            jnp.concatenate(
                [
                    total[group, pl.ds(first + item, steps, stride=loads), :]
                    for item in range(share)
                ],
                0,
            )
            for group in range(groups)
        ]
        chunk = jnp.concatenate(columns, 1)
        if index > 0:
            chunk, power = scaled(chunk)
        else:
            power = jnp.full((1, 1), HEADROOM, F32)
        out[: share * steps] = chunk
        out[row : row + 1] = jnp.broadcast_to(power, (1, groups * LANES))


def far_first_kernel(
    span, couplings, share, sources, ratio, counts, offsets, past, kernels, *refs
):
    (*outs, tail, history, kernel_buffer, total, scalars, sems, past_sem, scalar_sem) = refs
    fetched = pltpu.make_async_copy(past, history, past_sem)
    listed = pltpu.make_async_copy(offsets, scalars, scalar_sem)
    listed.start()
    fetched.start()
    start_slots(counts, kernels, kernel_buffer, sems)
    steps = history.shape[0] - span
    loads = history.shape[1]
    groups = total.shape[0]
    rows = groups * LANES
    size = share * steps
    listed.wait()
    fetched.wait()
    tail[...] = history[steps:]

    def arrived(slot):
        pltpu.make_async_copy(
            kernels.at[slot], kernel_buffer.at[slot], sems.at[slot]
        ).wait()

    sum_slots(counts, scalars, history, kernel_buffer, total, span, arrived)
    for out in outs:
        out[size:] = jnp.zeros_like(out[size:])
    write_chunks(total, outs, share, loads, size + share * couplings)
    target, source = lax.axis_index("tgt"), lax.axis_index("src")
    holds = source == target // ratio
    at = pl.multiple_of(target % ratio * rows, LANES)
    recent = history[history.shape[0] - couplings :, :, pl.ds(at, rows)].astype(F32)
    recent = jnp.where(holds, recent, jnp.zeros_like(recent)).reshape(couplings * loads, rows)
    for group in range(groups):
        total[group, : couplings * loads] = recent[:, group * LANES : (group + 1) * LANES]
    for index, out in enumerate(outs):
        first = partner(source, index, sources) * share % loads
        for item in range(share):
            for step in range(couplings):
                row = size + item * couplings + step
                for group in range(groups):
                    out[row : row + 1, group * LANES : (group + 1) * LANES] = total[
                        group, pl.ds(step * loads + first + item, 1), :
                    ]


def far_next_kernel(table, span, share, ratio, counts, offsets, tail, kernels, *refs):
    sources = len(table)
    arrived, refs = refs[: sources * ratio], refs[sources * ratio :]
    (*outs, total, strided, history) = refs
    steps = history.shape[0] - span
    loads, columns = history.shape[1:]
    groups = total.shape[0]
    history[:span] = tail[...]
    target, source = lax.axis_index("tgt"), lax.axis_index("src")
    chip, own = target // ratio, lax.rem(target, ratio)
    for index in range(sources):
        first = 0
        for plane in range(sources):
            for one in range(sources):
                here = partner(table[plane][one], index, sources)
                first = jnp.where(
                    (source == plane) & (chip == here), one * share % loads, first
                )
        for turn in range(ratio):
            chunk = arrived[turn * sources + index]
            part = lax.rem(own + ratio - turn, ratio)
            for item in range(share):
                for group in range(groups):
                    strided[
                        part * groups + group,
                        pl.ds(first + item, steps, stride=loads),
                        :,
                    ] = chunk[
                        item * steps : (item + 1) * steps, group * LANES : (group + 1) * LANES
                    ].astype(F32)
    for group in range(columns // LANES):
        history[span:, :, group * LANES : (group + 1) * LANES] = (
            strided[group].reshape(steps, loads, LANES).astype(BF16)
        )
    sum_slots(counts, offsets, history, kernels, total, span)
    write_chunks(total, outs, share, loads, share * steps)


def prepare_kernel(levels, couplings, inverse, *refs):
    (
        inverse_high,
        inverse_low,
        coupling_high,
        coupling_low,
        first_high,
        first_low,
        *powers,
        matrix,
    ) = refs
    count, rows, _ = couplings.shape
    high, low = split(inverse[...])
    inverse_high[...] = high
    inverse_low[...] = low
    matrix[...] = jnp.zeros_like(matrix)
    identity = (
        lax.broadcasted_iota(jnp.int32, (rows, rows), 0)
        == lax.broadcasted_iota(jnp.int32, (rows, rows), 1)
    ).astype(F32)
    for lag in range(count):
        coupling_high[lag], coupling_low[lag] = split(couplings[lag])
        matrix[lag * rows : (lag + 1) * rows, :rows] = -dot3(couplings[lag], high, low)
        if lag + 1 < count:
            matrix[
                lag * rows : (lag + 1) * rows, (lag + 1) * rows : (lag + 2) * rows
            ] = identity
    first_high[...], first_low[...] = split(matrix[:rows, :rows])
    power_high, power_low = split(matrix[...])
    for level in range(1, levels):
        wide = powers[2 * (level - 1)].shape[1]
        if level == 1 and wide == count * rows:
            column = matrix[:, :rows]
            product = dot3(column, first_high[...], first_low[...])
            product += jnp.concatenate([column[rows:], jnp.zeros((rows, rows), F32)], 0)
            product = jnp.concatenate([product, matrix[:, : wide - rows]], 1)
        else:
            product = dot3(matrix[...], power_high[:, :wide], power_low[:, :wide])
        power_high, power_low = split(product)
        powers[2 * (level - 1)][...] = power_high
        powers[2 * (level - 1) + 1][...] = power_low
        if level + 1 < levels:
            matrix[...] = product


def solve_kernel(steps, share, levels, parts, packed, *refs):
    partials, refs = refs[:parts], refs[parts:]
    (
        driving,
        earlier,
        inverse_high,
        inverse_low,
        coupling_high,
        coupling_low,
        first_high,
        first_low,
        *powers,
    ) = refs[: 8 + 2 * (levels - 1)]
    solved, sent, *following = refs[8 + 2 * (levels - 1) :]
    count, rows, _ = coupling_high.shape
    size = share * steps
    power_row = size + share * count if packed else size
    adjusted = driving[...].astype(F32)
    for partial in partials:
        adjusted = adjusted - unscaled(partial, size, power_row)
    row_of = lax.broadcasted_iota(jnp.int32, (size, 1), 0)
    padded = -(-share // SUBLANES) * SUBLANES
    if packed:
        known = partials[0][size:]
        for partial in partials[1:]:
            known = known + partial[size:]
    else:
        known = earlier[...]

    def back(lag):
        pieces = [
            known[item * count + count - lag : item * count + count - lag + 1]
            for item in range(share)
        ]
        pieces.append(jnp.zeros((padded - share, rows), F32))
        return jnp.concatenate(pieces, 0)

    for step in range(count):
        pull = None
        for lag in range(step + 1, count + 1):
            term = dot3(back(lag - step), coupling_high[lag - 1], coupling_low[lag - 1])
            pull = term if pull is None else pull + term
        for item in range(share):
            adjusted = adjusted - jnp.where(
                row_of == item * steps + step, pull[item : item + 1], 0.0
            )
    within = row_of % steps
    driven = dot3(adjusted, inverse_high[...], inverse_low[...])

    def delayed(value, delay):
        return jnp.where(within >= delay, pltpu.roll(value, delay, 0), 0.0)

    columns = [driven + delayed(dot3(driven, first_high[...], first_low[...]), 1)]
    if count > 1:
        columns.append(delayed(driven, 1))
    columns += [jnp.zeros_like(driven)] * (count - 2)
    total = jnp.concatenate(columns, 1)
    for level in range(1, levels):
        high, low = powers[2 * (level - 1)], powers[2 * (level - 1) + 1]
        wide = high.shape[1]
        total = total[:, :wide] + delayed(dot3(total, high[...], low[...]), 2**level)
    result = total[:, :rows]
    solved[...] = result
    sent[:size], power = scaled(result)
    sent[size:] = jnp.broadcast_to(power, (sent.shape[0] - size, rows))
    if following:
        rounded, state = following
        rounded[...] = result.astype(BF16)
        state[...] = jnp.zeros_like(state)
        for item in range(share):
            state[item * count : (item + 1) * count] = result[
                (item + 1) * steps - count : (item + 1) * steps
            ]


def spread_kernel(block, share, own, *refs):
    (*chunks, out, strided, ready, sem) = refs
    steps, loads, rows = ready.shape
    sources = (len(chunks) + 1) if block == 0 else len(chunks)
    size = share * steps
    source = lax.axis_index("src")
    for index, chunk in enumerate([own, *chunks][:sources]):
        first = sender(source, index, sources) * share % loads
        value = chunk[...] if index == 0 else unscaled(chunk, size, size)
        for item in range(share):
            for group in range(rows // LANES):
                strided[group, pl.ds(first + item, steps, stride=loads), :] = value[
                    item * steps : (item + 1) * steps, group * LANES : (group + 1) * LANES
                ]
    for group in range(rows // LANES):
        ready[:, :, group * LANES : (group + 1) * LANES] = strided[group].reshape(
            steps, loads, LANES
        )
    copy = pltpu.make_async_copy(ready, out.at[pl.ds(block * steps, steps)], sem)
    copy.start()
    copy.wait()


def landing(plane, sources):
    shares = sorted(range(sources), key=lambda z: (-abs(z - plane), z))
    if sources & (sources - 1) == 0:
        chips = sorted(range(sources), key=lambda e: (bin(e ^ plane).count("1"), e))
    else:
        chips = sorted(range(sources), key=lambda e: (abs(e - plane), e))
    where = [0] * sources
    for one, chip in zip(shares, chips):
        where[one] = chip
    return where


def local(incident, past_density, kernels, lag_offset, lag_counts, couplings, inverse):
    all_steps, loads, rows = incident.shape
    columns = past_density.shape[2]
    slots = kernels.shape[0]
    span = lag_offset.shape[2]
    steps = past_density.shape[0] - span
    blocks = all_steps // steps
    count = couplings.shape[0]
    levels = steps.bit_length() - 1
    ratio = columns // rows
    sources = lax.axis_size("src")
    targets = lax.axis_size("tgt")
    target = lax.axis_index("tgt")
    source = lax.axis_index("src")
    share = max(loads // sources, 1)
    size = share * steps
    groups = rows // LANES
    pad = -(-(share * count + 1) // SUBLANES) * SUBLANES

    table = [landing(plane, sources) for plane in range(sources)]

    def params(mebibytes):
        return pltpu.CompilerParams(vmem_limit_bytes=mebibytes * 2**20)

    def cost(work):
        return pl.CostEstimate(flops=work * 10**9, bytes_accessed=0, transcendentals=0)

    def trade(value, shift):
        pairs = [(i, partner(i, shift, sources)) for i in range(sources)]
        return lax.ppermute(value, "src", pairs)

    def trade_each(values):
        return [
            trade(value.astype(jnp.float16), k).astype(F32)
            for k, value in enumerate(values, 1)
        ]

    prepared = pl.pallas_call(
        functools.partial(prepare_kernel, levels),
        out_shape=[jax.ShapeDtypeStruct((rows, rows), BF16)] * 2
        + [jax.ShapeDtypeStruct((count, rows, rows), BF16)] * 2
        + [jax.ShapeDtypeStruct((rows, rows), BF16)] * 2
        + [jax.ShapeDtypeStruct((count * rows, count * rows), BF16)] * (2 * (levels - 2))
        + [jax.ShapeDtypeStruct((count * rows, rows), BF16)] * 2,
        in_specs=[VMEM, VMEM],
        out_specs=[VMEM] * (6 + 2 * (levels - 1)),
        scratch_shapes=[pltpu.VMEM((count * rows, count * rows), F32)],
        compiler_params=params(16),
        cost_estimate=cost(5),
        name="prepare",
    )(couplings, inverse)

    def solve(partials, driving, earlier, first, last):
        operands = [*partials, driving, earlier, *prepared]
        shapes = [
            jax.ShapeDtypeStruct((size, rows), F32),
            jax.ShapeDtypeStruct((size + SUBLANES, rows), F32),
        ]
        if not last:
            shapes.append(jax.ShapeDtypeStruct((size, rows), BF16))
            shapes.append(jax.ShapeDtypeStruct((pad, rows), F32))
        return pl.pallas_call(
            functools.partial(solve_kernel, steps, share, levels, len(partials), first),
            out_shape=shapes,
            in_specs=[VMEM] * len(operands),
            out_specs=[VMEM] * len(shapes),
            compiler_params=params(12),
            cost_estimate=cost(3),
            name="solve",
        )(*operands)

    def spread(block, before, own, chunks):
        last = [] if block == 0 else [before]
        return pl.pallas_call(
            functools.partial(spread_kernel, block, share),
            out_shape=jax.ShapeDtypeStruct((all_steps, loads, rows), F32),
            in_specs=[VMEM] * sources + [HBM] * len(last),
            out_specs=HBM,
            scratch_shapes=[
                pltpu.VMEM((groups, steps * loads, LANES), F32),
                pltpu.VMEM((steps, loads, rows), F32),
                pltpu.SemaphoreType.DMA,
            ],
            input_output_aliases={sources: 0} if last else {},
            compiler_params=params(8),
            name="spread",
        )(own, *chunks, *last)

    own_incident = lax.dynamic_slice_in_dim(incident, source * share % loads, share, 1)
    own_incident = own_incident.reshape(blocks, steps, share, rows)
    own_incident = own_incident.transpose(0, 2, 1, 3).reshape(blocks, size, rows)

    total_scratch = pltpu.VMEM((groups, steps * loads, LANES), F32)
    history_scratch = pltpu.VMEM((span + steps, loads, columns), BF16)

    *partials, tail = pl.pallas_call(
        functools.partial(far_first_kernel, span, count, share, sources, ratio),
        out_shape=[jax.ShapeDtypeStruct((size + pad, rows), F32)] * sources
        + [jax.ShapeDtypeStruct((span, loads, columns), BF16)],
        in_specs=[SMEM, HBM, HBM, HBM],
        out_specs=[VMEM] * (sources + 1),
        scratch_shapes=[
            history_scratch,
            pltpu.VMEM(kernels.shape, BF16),
            total_scratch,
            pltpu.SMEM(lag_offset.shape, jnp.int32),
            pltpu.SemaphoreType.DMA((slots,)),
            pltpu.SemaphoreType.DMA,
            pltpu.SemaphoreType.DMA,
        ],
        compiler_params=params(53),
        cost_estimate=cost(2),
        name="far_first",
    )(lag_counts, lag_offset, past_density, kernels)

    state = jnp.zeros((pad, rows), F32)
    output = None
    for block in range(blocks):
        if block > 0:
            moves = [
                (
                    (one * ratio + part) * sources + z,
                    (table[one][z] * ratio + part) * sources + one,
                )
                for one in range(sources)
                for part in range(ratio)
                for z in range(sources)
            ]
            landed = lax.ppermute(rounded, ("tgt", "src"), moves)
            chunks = trade_each([sent] * (sources - 1))
            arrived = [landed]
            for k in range(1, sources):
                pairs = [
                    (e * ratio + part, partner(e, k, sources) * ratio + part)
                    for e in range(sources)
                    for part in range(ratio)
                ]
                arrived.append(lax.ppermute(landed, "tgt", pairs))
            swapped = []
            for turn in range(1, ratio):
                pairs = [
                    (e * ratio + part, e * ratio + (part + turn) % ratio)
                    for e in range(sources)
                    for part in range(ratio)
                ]
                swapped += [lax.ppermute(chunk, "tgt", pairs) for chunk in arrived]
            partials = pl.pallas_call(
                functools.partial(far_next_kernel, table, span, share, ratio),
                out_shape=[jax.ShapeDtypeStruct((size + SUBLANES, rows), F32)] * sources,
                in_specs=[SMEM, SMEM, VMEM, VMEM] + [VMEM] * (sources * ratio),
                out_specs=[VMEM] * sources,
                scratch_shapes=[
                    total_scratch,
                    pltpu.VMEM((columns // LANES, steps * loads, LANES), F32),
                    history_scratch,
                ],
                compiler_params=params(12),
                cost_estimate=cost(3),
                name="far_next",
            )(lag_counts, lag_offset, tail, kernels, *arrived, *swapped)
            output = spread(block - 1, output, solved, chunks)
        received = [partials[0]] + trade_each(partials[1:])
        solved, sent, *following = solve(
            received, own_incident[block], state, block == 0, block + 1 == blocks
        )
        if following:
            rounded, state = following
    return spread(blocks - 1, output, solved, trade_each([sent] * (sources - 1)))


def solution(mesh):
    return jax.shard_map(
        local,
        mesh=mesh,
        in_specs=(
            P(None, None, "tgt"),
            P(None, None, "src"),
            P(None, "src", "tgt"),
            P("tgt", "src", None),
            P("tgt", "src"),
            P(None, "tgt", None),
            P("tgt", None),
        ),
        out_specs=P(None, None, "tgt"),
        check_vma=False,
    )
```

```python
import functools

import jax
import jax.numpy as jnp
from jax import lax
from jax.experimental import pallas as pl
from jax.experimental.pallas import tpu as pltpu
from jax.sharding import PartitionSpec as P

F32 = jnp.float32
BF16 = jnp.bfloat16
LANES = 128
SUBLANES = 8
VMEM = pl.BlockSpec(memory_space=pltpu.VMEM)
SMEM = pl.BlockSpec(memory_space=pltpu.SMEM)
HBM = pl.BlockSpec(memory_space=pltpu.HBM)


def partner(index, shift, count):
    if count & (count - 1) == 0:
        return index ^ shift
    return (index + shift) % count


def sender(index, shift, count):
    if count & (count - 1) == 0:
        return index ^ shift
    return (index - shift) % count


def split(value):
    high = value.astype(BF16)
    return high, (value - high.astype(F32)).astype(BF16)


def dot3(value, high, low):
    rows = value.shape[0]
    value_high, value_low = split(value)
    both = jnp.dot(
        jnp.concatenate([value_high, value_low], 0), high, preferred_element_type=F32
    )
    cross = jnp.dot(value_high, low, preferred_element_type=F32)
    return both[:rows] + (both[rows:] + cross)


HEADROOM = 13.0
SMALLEST = 2.0**-100


def scaled(chunk):
    largest = jnp.max(jnp.max(jnp.abs(chunk), axis=0, keepdims=True), axis=1, keepdims=True)
    power = jnp.floor(jnp.log2(jnp.maximum(largest, SMALLEST)))
    return chunk * jnp.exp2(HEADROOM - power), power


def unscaled(packed, size, row):
    return packed[:size] * jnp.exp2(packed[row : row + 1] - HEADROOM)


def start_slots(counts, kernels, kernel_buffer, sems):
    for slot in range(kernel_buffer.shape[0]):

        @pl.when(slot < counts[0, 0])
        def _():
            pltpu.make_async_copy(
                kernels.at[slot], kernel_buffer.at[slot], sems.at[slot]
            ).start()


def sum_slots(counts, offsets, history, kernels, total, span, arrived=None):
    steps = history.shape[0] - span
    loads, columns = history.shape[1:]
    count = counts[0, 0]
    total[...] = jnp.zeros_like(total)

    def window(slot):
        taken = history[pl.ds(span - offsets[0, 0, slot], steps)]
        return taken.reshape(steps * loads, columns)

    def add(first, together):
        if arrived is not None:
            for slot in range(together):
                arrived(first + slot)
        windows = jnp.concatenate([window(first + slot) for slot in range(together)], 1)
        matrix = kernels[pl.ds(first, together)].reshape(together * columns, -1)
        product = jnp.dot(windows, matrix, preferred_element_type=F32)
        for group in range(total.shape[0]):
            total[group] += product[:, group * LANES : (group + 1) * LANES]

    done = 0
    together = 1 << (kernels.shape[0].bit_length() - 1)
    while together:
        rounds = (count - done) // together

        def step(index, carry, first=done, together=together):
            add(first + index * together, together)
            return carry

        lax.fori_loop(0, rounds, step, 0)
        done += rounds * together
        together //= 2


def write_chunks(total, outs, share, loads, row):
    groups, size, _ = total.shape
    steps = size // loads
    source, sources = lax.axis_index("src"), len(outs)
    for index, out in enumerate(outs):
        first = partner(source, index, sources) * share % loads
        columns = [
            jnp.concatenate(
                [
                    total[group, pl.ds(first + item, steps, stride=loads), :]
                    for item in range(share)
                ],
                0,
            )
            for group in range(groups)
        ]
        chunk = jnp.concatenate(columns, 1)
        if index > 0:
            chunk, power = scaled(chunk)
        else:
            power = jnp.full((1, 1), HEADROOM, F32)
        out[: share * steps] = chunk
        out[row : row + 1] = jnp.broadcast_to(power, (1, groups * LANES))


def far_first_kernel(
    span, couplings, share, sources, ratio, counts, offsets, past, kernels, *refs
):
    (*outs, tail, history, kernel_buffer, total, scalars, sems, past_sem, scalar_sem) = refs
    fetched = pltpu.make_async_copy(past, history, past_sem)
    listed = pltpu.make_async_copy(offsets, scalars, scalar_sem)
    listed.start()
    fetched.start()
    start_slots(counts, kernels, kernel_buffer, sems)
    steps = history.shape[0] - span
    loads = history.shape[1]
    groups = total.shape[0]
    rows = groups * LANES
    size = share * steps
    listed.wait()
    fetched.wait()
    tail[...] = history[steps:]

    def arrived(slot):
        pltpu.make_async_copy(
            kernels.at[slot], kernel_buffer.at[slot], sems.at[slot]
        ).wait()

    sum_slots(counts, scalars, history, kernel_buffer, total, span, arrived)
    for out in outs:
        out[size:] = jnp.zeros_like(out[size:])
    write_chunks(total, outs, share, loads, size + share * couplings)
    target, source = lax.axis_index("tgt"), lax.axis_index("src")
    holds = source == target // ratio
    at = pl.multiple_of(target % ratio * rows, LANES)
    recent = history[history.shape[0] - couplings :, :, pl.ds(at, rows)].astype(F32)
    recent = jnp.where(holds, recent, jnp.zeros_like(recent)).reshape(couplings * loads, rows)
    for group in range(groups):
        total[group, : couplings * loads] = recent[:, group * LANES : (group + 1) * LANES]
    for index, out in enumerate(outs):
        first = partner(source, index, sources) * share % loads
        for item in range(share):
            for step in range(couplings):
                row = size + item * couplings + step
                for group in range(groups):
                    out[row : row + 1, group * LANES : (group + 1) * LANES] = total[
                        group, pl.ds(step * loads + first + item, 1), :
                    ]


def far_next_kernel(table, span, share, ratio, counts, offsets, tail, kernels, *refs):
    sources = len(table)
    arrived, refs = refs[: sources * ratio], refs[sources * ratio :]
    (*outs, total, strided, history) = refs
    steps = history.shape[0] - span
    loads, columns = history.shape[1:]
    groups = total.shape[0]
    history[:span] = tail[...]
    target, source = lax.axis_index("tgt"), lax.axis_index("src")
    chip, own = target // ratio, lax.rem(target, ratio)
    for index in range(sources):
        first = 0
        for plane in range(sources):
            for one in range(sources):
                here = partner(table[plane][one], index, sources)
                first = jnp.where(
                    (source == plane) & (chip == here), one * share % loads, first
                )
        for turn in range(ratio):
            chunk = arrived[turn * sources + index]
            part = lax.rem(own + ratio - turn, ratio)
            for item in range(share):
                for group in range(groups):
                    strided[
                        part * groups + group,
                        pl.ds(first + item, steps, stride=loads),
                        :,
                    ] = chunk[
                        item * steps : (item + 1) * steps, group * LANES : (group + 1) * LANES
                    ].astype(F32)
    for group in range(columns // LANES):
        history[span:, :, group * LANES : (group + 1) * LANES] = (
            strided[group].reshape(steps, loads, LANES).astype(BF16)
        )
    sum_slots(counts, offsets, history, kernels, total, span)
    write_chunks(total, outs, share, loads, share * steps)


def prepare_kernel(levels, couplings, inverse, *refs):
    (
        inverse_high,
        inverse_low,
        coupling_high,
        coupling_low,
        first_high,
        first_low,
        *powers,
        matrix,
    ) = refs
    count, rows, _ = couplings.shape
    high, low = split(inverse[...])
    inverse_high[...] = high
    inverse_low[...] = low
    matrix[...] = jnp.zeros_like(matrix)
    identity = (
        lax.broadcasted_iota(jnp.int32, (rows, rows), 0)
        == lax.broadcasted_iota(jnp.int32, (rows, rows), 1)
    ).astype(F32)
    for lag in range(count):
        coupling_high[lag], coupling_low[lag] = split(couplings[lag])
        matrix[lag * rows : (lag + 1) * rows, :rows] = -dot3(couplings[lag], high, low)
        if lag + 1 < count:
            matrix[
                lag * rows : (lag + 1) * rows, (lag + 1) * rows : (lag + 2) * rows
            ] = identity
    first_high[...], first_low[...] = split(matrix[:rows, :rows])
    power_high, power_low = split(matrix[...])
    for level in range(1, levels):
        wide = powers[2 * (level - 1)].shape[1]
        if level == 1 and wide == count * rows:
            column = matrix[:, :rows]
            product = dot3(column, first_high[...], first_low[...])
            product += jnp.concatenate([column[rows:], jnp.zeros((rows, rows), F32)], 0)
            product = jnp.concatenate([product, matrix[:, : wide - rows]], 1)
        else:
            product = dot3(matrix[...], power_high[:, :wide], power_low[:, :wide])
        power_high, power_low = split(product)
        powers[2 * (level - 1)][...] = power_high
        powers[2 * (level - 1) + 1][...] = power_low
        if level + 1 < levels:
            matrix[...] = product


def solve_kernel(steps, share, levels, parts, packed, *refs):
    partials, refs = refs[:parts], refs[parts:]
    (
        driving,
        earlier,
        inverse_high,
        inverse_low,
        coupling_high,
        coupling_low,
        first_high,
        first_low,
        *powers,
    ) = refs[: 8 + 2 * (levels - 1)]
    solved, sent, *following = refs[8 + 2 * (levels - 1) :]
    count, rows, _ = coupling_high.shape
    size = share * steps
    power_row = size + share * count if packed else size
    adjusted = driving[...].astype(F32)
    for partial in partials:
        adjusted = adjusted - unscaled(partial, size, power_row)
    row_of = lax.broadcasted_iota(jnp.int32, (size, 1), 0)
    padded = -(-share // SUBLANES) * SUBLANES
    if packed:
        known = partials[0][size:]
        for partial in partials[1:]:
            known = known + partial[size:]
    else:
        known = earlier[...]

    def back(lag):
        pieces = [
            known[item * count + count - lag : item * count + count - lag + 1]
            for item in range(share)
        ]
        pieces.append(jnp.zeros((padded - share, rows), F32))
        return jnp.concatenate(pieces, 0)

    for step in range(count):
        pull = None
        for lag in range(step + 1, count + 1):
            term = dot3(back(lag - step), coupling_high[lag - 1], coupling_low[lag - 1])
            pull = term if pull is None else pull + term
        for item in range(share):
            adjusted = adjusted - jnp.where(
                row_of == item * steps + step, pull[item : item + 1], 0.0
            )
    within = row_of % steps
    driven = dot3(adjusted, inverse_high[...], inverse_low[...])

    def delayed(value, delay):
        return jnp.where(within >= delay, pltpu.roll(value, delay, 0), 0.0)

    columns = [driven + delayed(dot3(driven, first_high[...], first_low[...]), 1)]
    if count > 1:
        columns.append(delayed(driven, 1))
    columns += [jnp.zeros_like(driven)] * (count - 2)
    total = jnp.concatenate(columns, 1)
    for level in range(1, levels):
        high, low = powers[2 * (level - 1)], powers[2 * (level - 1) + 1]
        wide = high.shape[1]
        total = total[:, :wide] + delayed(dot3(total, high[...], low[...]), 2**level)
    result = total[:, :rows]
    solved[...] = result
    sent[:size], power = scaled(result)
    sent[size:] = jnp.broadcast_to(power, (sent.shape[0] - size, rows))
    if following:
        rounded, state = following
        rounded[...] = result.astype(BF16)
        state[...] = jnp.zeros_like(state)
        for item in range(share):
            state[item * count : (item + 1) * count] = result[
                (item + 1) * steps - count : (item + 1) * steps
            ]


def spread_kernel(block, share, own, *refs):
    (*chunks, out, ready, sems) = refs
    groups, steps, loads, _ = ready.shape
    sources = (len(chunks) + 1) if block == 0 else len(chunks)
    size = share * steps
    source = lax.axis_index("src")
    rows_of = ready.reshape(groups, steps * loads, LANES)
    copies = []
    for group in range(groups):
        lanes = slice(group * LANES, (group + 1) * LANES)
        for index, chunk in enumerate([own, *chunks][:sources]):
            first = sender(source, index, sources) * share % loads
            value = chunk[:size, lanes]
            if index > 0:
                value = value * jnp.exp2(chunk[size : size + 1, lanes] - HEADROOM)
            for item in range(share):
                rows_of[group, pl.ds(first + item, steps, stride=loads), :] = value[
                    item * steps : (item + 1) * steps
                ]
        copies.append(
            pltpu.make_async_copy(
                ready.at[group],
                out.at[pl.ds(block * steps, steps), :, pl.ds(group * LANES, LANES)],
                sems.at[group],
            )
        )
        copies[-1].start()
    for copy in copies:
        copy.wait()


def landing(plane, sources):
    shares = sorted(range(sources), key=lambda z: (-abs(z - plane), z))
    if sources & (sources - 1) == 0:
        chips = sorted(range(sources), key=lambda e: (bin(e ^ plane).count("1"), e))
    else:
        chips = sorted(range(sources), key=lambda e: (abs(e - plane), e))
    where = [0] * sources
    for one, chip in zip(shares, chips):
        where[one] = chip
    return where


def local(incident, past_density, kernels, lag_offset, lag_counts, couplings, inverse):
    all_steps, loads, rows = incident.shape
    columns = past_density.shape[2]
    slots = kernels.shape[0]
    span = lag_offset.shape[2]
    steps = past_density.shape[0] - span
    blocks = all_steps // steps
    count = couplings.shape[0]
    levels = steps.bit_length() - 1
    ratio = columns // rows
    sources = lax.axis_size("src")
    targets = lax.axis_size("tgt")
    target = lax.axis_index("tgt")
    source = lax.axis_index("src")
    share = max(loads // sources, 1)
    size = share * steps
    groups = rows // LANES
    pad = -(-(share * count + 1) // SUBLANES) * SUBLANES

    table = [landing(plane, sources) for plane in range(sources)]

    def params(mebibytes):
        return pltpu.CompilerParams(vmem_limit_bytes=mebibytes * 2**20)

    def cost(work):
        return pl.CostEstimate(flops=work * 10**9, bytes_accessed=0, transcendentals=0)

    def trade(value, shift):
        pairs = [(i, partner(i, shift, sources)) for i in range(sources)]
        return lax.ppermute(value, "src", pairs)

    def trade_each(values):
        return [
            trade(value.astype(jnp.float16), k).astype(F32)
            for k, value in enumerate(values, 1)
        ]

    prepared = pl.pallas_call(
        functools.partial(prepare_kernel, levels),
        out_shape=[jax.ShapeDtypeStruct((rows, rows), BF16)] * 2
        + [jax.ShapeDtypeStruct((count, rows, rows), BF16)] * 2
        + [jax.ShapeDtypeStruct((rows, rows), BF16)] * 2
        + [jax.ShapeDtypeStruct((count * rows, count * rows), BF16)] * (2 * (levels - 2))
        + [jax.ShapeDtypeStruct((count * rows, rows), BF16)] * 2,
        in_specs=[VMEM, VMEM],
        out_specs=[VMEM] * (6 + 2 * (levels - 1)),
        scratch_shapes=[pltpu.VMEM((count * rows, count * rows), F32)],
        compiler_params=params(16),
        cost_estimate=cost(5),
        name="prepare",
    )(couplings, inverse)

    def solve(partials, driving, earlier, first, last):
        operands = [*partials, driving, earlier, *prepared]
        shapes = [
            jax.ShapeDtypeStruct((size, rows), F32),
            jax.ShapeDtypeStruct((size + SUBLANES, rows), F32),
        ]
        if not last:
            shapes.append(jax.ShapeDtypeStruct((size, rows), BF16))
            shapes.append(jax.ShapeDtypeStruct((pad, rows), F32))
        return pl.pallas_call(
            functools.partial(solve_kernel, steps, share, levels, len(partials), first),
            out_shape=shapes,
            in_specs=[VMEM] * len(operands),
            out_specs=[VMEM] * len(shapes),
            compiler_params=params(12),
            cost_estimate=cost(3),
            name="solve",
        )(*operands)

    def spread(block, before, own, chunks):
        last = [] if block == 0 else [before]
        return pl.pallas_call(
            functools.partial(spread_kernel, block, share),
            out_shape=jax.ShapeDtypeStruct((all_steps, loads, rows), F32),
            in_specs=[VMEM] * sources + [HBM] * len(last),
            out_specs=HBM,
            scratch_shapes=[
                pltpu.VMEM((groups, steps, loads, LANES), F32),
                pltpu.SemaphoreType.DMA((groups,)),
            ],
            input_output_aliases={sources: 0} if last else {},
            compiler_params=params(8),
            name="spread",
        )(own, *chunks, *last)

    own_incident = lax.dynamic_slice_in_dim(incident, source * share % loads, share, 1)
    own_incident = own_incident.reshape(blocks, steps, share, rows)
    own_incident = own_incident.transpose(0, 2, 1, 3).reshape(blocks, size, rows)

    total_scratch = pltpu.VMEM((groups, steps * loads, LANES), F32)
    history_scratch = pltpu.VMEM((span + steps, loads, columns), BF16)

    *partials, tail = pl.pallas_call(
        functools.partial(far_first_kernel, span, count, share, sources, ratio),
        out_shape=[jax.ShapeDtypeStruct((size + pad, rows), F32)] * sources
        + [jax.ShapeDtypeStruct((span, loads, columns), BF16)],
        in_specs=[SMEM, HBM, HBM, HBM],
        out_specs=[VMEM] * (sources + 1),
        scratch_shapes=[
            history_scratch,
            pltpu.VMEM(kernels.shape, BF16),
            total_scratch,
            pltpu.SMEM(lag_offset.shape, jnp.int32),
            pltpu.SemaphoreType.DMA((slots,)),
            pltpu.SemaphoreType.DMA,
            pltpu.SemaphoreType.DMA,
        ],
        compiler_params=params(53),
        cost_estimate=cost(2),
        name="far_first",
    )(lag_counts, lag_offset, past_density, kernels)

    state = jnp.zeros((pad, rows), F32)
    output = None
    for block in range(blocks):
        if block > 0:
            moves = [
                (
                    (one * ratio + part) * sources + z,
                    (table[one][z] * ratio + part) * sources + one,
                )
                for one in range(sources)
                for part in range(ratio)
                for z in range(sources)
            ]
            landed = lax.ppermute(rounded, ("tgt", "src"), moves)
            chunks = trade_each([sent] * (sources - 1))
            arrived = [landed]
            for k in range(1, sources):
                pairs = [
                    (e * ratio + part, partner(e, k, sources) * ratio + part)
                    for e in range(sources)
                    for part in range(ratio)
                ]
                arrived.append(lax.ppermute(landed, "tgt", pairs))
            swapped = []
            for turn in range(1, ratio):
                pairs = [
                    (e * ratio + part, e * ratio + (part + turn) % ratio)
                    for e in range(sources)
                    for part in range(ratio)
                ]
                swapped += [lax.ppermute(chunk, "tgt", pairs) for chunk in arrived]
            partials = pl.pallas_call(
                functools.partial(far_next_kernel, table, span, share, ratio),
                out_shape=[jax.ShapeDtypeStruct((size + SUBLANES, rows), F32)] * sources,
                in_specs=[SMEM, SMEM, VMEM, VMEM] + [VMEM] * (sources * ratio),
                out_specs=[VMEM] * sources,
                scratch_shapes=[
                    total_scratch,
                    pltpu.VMEM((columns // LANES, steps * loads, LANES), F32),
                    history_scratch,
                ],
                compiler_params=params(12),
                cost_estimate=cost(3),
                name="far_next",
            )(lag_counts, lag_offset, tail, kernels, *arrived, *swapped)
            output = spread(block - 1, output, solved, chunks)
        received = [partials[0]] + trade_each(partials[1:])
        solved, sent, *following = solve(
            received, own_incident[block], state, block == 0, block + 1 == blocks
        )
        if following:
            rounded, state = following
    return spread(blocks - 1, output, solved, trade_each([sent] * (sources - 1)))


def solution(mesh):
    return jax.shard_map(
        local,
        mesh=mesh,
        in_specs=(
            P(None, None, "tgt"),
            P(None, None, "src"),
            P(None, "src", "tgt"),
            P("tgt", "src", None),
            P("tgt", "src"),
            P(None, "tgt", None),
            P("tgt", None),
        ),
        out_specs=P(None, None, "tgt"),
        check_vma=False,
    )
```

```python
import functools

import jax
import jax.numpy as jnp
from jax import lax
from jax.experimental import pallas as pl
from jax.experimental.pallas import tpu as pltpu
from jax.sharding import PartitionSpec as P

F32 = jnp.float32
BF16 = jnp.bfloat16
LANES = 128
SUBLANES = 8
VMEM = pl.BlockSpec(memory_space=pltpu.VMEM)
SMEM = pl.BlockSpec(memory_space=pltpu.SMEM)
HBM = pl.BlockSpec(memory_space=pltpu.HBM)


def partner(index, shift, count):
    if count & (count - 1) == 0:
        return index ^ shift
    return (index + shift) % count


def sender(index, shift, count):
    if count & (count - 1) == 0:
        return index ^ shift
    return (index - shift) % count


def split(value):
    high = value.astype(BF16)
    return high, (value - high.astype(F32)).astype(BF16)


def dot3(value, high, low):
    rows = value.shape[0]
    value_high, value_low = split(value)
    both = jnp.dot(
        jnp.concatenate([value_high, value_low], 0), high, preferred_element_type=F32
    )
    cross = jnp.dot(value_high, low, preferred_element_type=F32)
    return both[:rows] + (both[rows:] + cross)


HEADROOM = 13.0
SMALLEST = 2.0**-100


def scaled(chunk):
    largest = jnp.max(jnp.max(jnp.abs(chunk), axis=0, keepdims=True), axis=1, keepdims=True)
    power = jnp.floor(jnp.log2(jnp.maximum(largest, SMALLEST)))
    return chunk * jnp.exp2(HEADROOM - power), power


def unscaled(packed, size, row):
    return packed[:size] * jnp.exp2(packed[row : row + 1] - HEADROOM)


def start_slots(counts, kernels, kernel_buffer, sems):
    for slot in range(kernel_buffer.shape[0]):

        @pl.when(slot < counts[0, 0])
        def _():
            pltpu.make_async_copy(
                kernels.at[slot], kernel_buffer.at[slot], sems.at[slot]
            ).start()


def sum_slots(counts, offsets, history, kernels, total, span, arrived=None):
    steps = history.shape[0] - span
    loads, columns = history.shape[1:]
    count = counts[0, 0]
    total[...] = jnp.zeros_like(total)

    def window(slot):
        taken = history[pl.ds(span - offsets[0, 0, slot], steps)]
        return taken.reshape(steps * loads, columns)

    def add(first, together):
        if arrived is not None:
            for slot in range(together):
                arrived(first + slot)
        windows = jnp.concatenate([window(first + slot) for slot in range(together)], 1)
        matrix = kernels[pl.ds(first, together)].reshape(together * columns, -1)
        product = jnp.dot(windows, matrix, preferred_element_type=F32)
        for group in range(total.shape[0]):
            total[group, : steps * loads] += product[:, group * LANES : (group + 1) * LANES]

    done = 0
    together = 1 << (kernels.shape[0].bit_length() - 1)
    while together:
        rounds = (count - done) // together

        def step(index, carry, first=done, together=together):
            add(first + index * together, together)
            return carry

        lax.fori_loop(0, rounds, step, 0)
        done += rounds * together
        together //= 2


def write_chunks(total, outs, share, loads, row):
    groups, size, _ = total.shape
    steps = size // loads - 1
    source, sources = lax.axis_index("src"), len(outs)
    for index, out in enumerate(outs):
        first = partner(source, index, sources) * share % loads
        columns = [
            jnp.concatenate(
                [
                    total[group, pl.ds(first + item, steps, stride=loads), :]
                    for item in range(share)
                ],
                0,
            )
            for group in range(groups)
        ]
        chunk = jnp.concatenate(columns, 1)
        if index > 0:
            chunk, power = scaled(chunk)
        else:
            power = jnp.full((1, 1), HEADROOM, F32)
        out[: share * steps] = chunk
        out[row : row + 1] = jnp.broadcast_to(power, (1, groups * LANES))


def far_first_kernel(
    span, couplings, share, sources, ratio, counts, offsets, past, kernels, *refs
):
    (*outs, tail, history, kernel_buffer, total, scalars, sems, past_sem, scalar_sem) = refs
    fetched = pltpu.make_async_copy(past, history, past_sem)
    listed = pltpu.make_async_copy(offsets, scalars, scalar_sem)
    listed.start()
    fetched.start()
    start_slots(counts, kernels, kernel_buffer, sems)
    steps = history.shape[0] - span
    loads = history.shape[1]
    groups = total.shape[0]
    rows = groups * LANES
    size = share * steps
    listed.wait()
    fetched.wait()
    tail[...] = history[steps:]

    def arrived(slot):
        pltpu.make_async_copy(
            kernels.at[slot], kernel_buffer.at[slot], sems.at[slot]
        ).wait()

    sum_slots(counts, scalars, history, kernel_buffer, total, span, arrived)
    for out in outs:
        out[size:] = jnp.zeros_like(out[size:])
    write_chunks(total, outs, share, loads, size + share * couplings)
    target, source = lax.axis_index("tgt"), lax.axis_index("src")
    holds = source == target // ratio
    at = pl.multiple_of(target % ratio * rows, LANES)
    recent = history[history.shape[0] - couplings :, :, pl.ds(at, rows)].astype(F32)
    recent = jnp.where(holds, recent, jnp.zeros_like(recent)).reshape(couplings * loads, rows)
    for group in range(groups):
        total[group, : couplings * loads] = recent[:, group * LANES : (group + 1) * LANES]
    for index, out in enumerate(outs):
        first = partner(source, index, sources) * share % loads
        for item in range(share):
            for step in range(couplings):
                row = size + item * couplings + step
                for group in range(groups):
                    out[row : row + 1, group * LANES : (group + 1) * LANES] = total[
                        group, pl.ds(step * loads + first + item, 1), :
                    ]


def far_next_kernel(table, span, share, ratio, counts, offsets, tail, kernels, *refs):
    sources = len(table)
    arrived, refs = refs[: sources * ratio], refs[sources * ratio :]
    (*outs, total, strided, history) = refs
    steps = history.shape[0] - span
    loads, columns = history.shape[1:]
    groups = total.shape[0]
    history[:span] = tail[...]
    target, source = lax.axis_index("tgt"), lax.axis_index("src")
    chip, own = target // ratio, lax.rem(target, ratio)
    for index in range(sources):
        first = 0
        for plane in range(sources):
            for one in range(sources):
                here = partner(table[plane][one], index, sources)
                first = jnp.where(
                    (source == plane) & (chip == here), one * share % loads, first
                )
        for turn in range(ratio):
            chunk = arrived[turn * sources + index]
            part = lax.rem(own + ratio - turn, ratio)
            for item in range(share):
                for group in range(groups):
                    strided[
                        part * groups + group,
                        pl.ds(first + item, steps, stride=loads),
                        :,
                    ] = chunk[
                        item * steps : (item + 1) * steps, group * LANES : (group + 1) * LANES
                    ].astype(F32)
    for group in range(columns // LANES):
        history[span:, :, group * LANES : (group + 1) * LANES] = (
            strided[group, : steps * loads].reshape(steps, loads, LANES).astype(BF16)
        )
    sum_slots(counts, offsets, history, kernels, total, span)
    write_chunks(total, outs, share, loads, share * steps)


def prepare_kernel(levels, couplings, inverse, *refs):
    (
        inverse_high,
        inverse_low,
        coupling_high,
        coupling_low,
        first_high,
        first_low,
        *powers,
        matrix,
    ) = refs
    count, rows, _ = couplings.shape
    high, low = split(inverse[...])
    inverse_high[...] = high
    inverse_low[...] = low
    matrix[...] = jnp.zeros_like(matrix)
    identity = (
        lax.broadcasted_iota(jnp.int32, (rows, rows), 0)
        == lax.broadcasted_iota(jnp.int32, (rows, rows), 1)
    ).astype(F32)
    for lag in range(count):
        coupling_high[lag], coupling_low[lag] = split(couplings[lag])
        matrix[lag * rows : (lag + 1) * rows, :rows] = -dot3(couplings[lag], high, low)
        if lag + 1 < count:
            matrix[
                lag * rows : (lag + 1) * rows, (lag + 1) * rows : (lag + 2) * rows
            ] = identity
    first_high[...], first_low[...] = split(matrix[:rows, :rows])
    power_high, power_low = split(matrix[...])
    for level in range(1, levels):
        wide = powers[2 * (level - 1)].shape[1]
        if level == 1 and wide == count * rows:
            column = matrix[:, :rows]
            product = dot3(column, first_high[...], first_low[...])
            product += jnp.concatenate([column[rows:], jnp.zeros((rows, rows), F32)], 0)
            product = jnp.concatenate([product, matrix[:, : wide - rows]], 1)
        else:
            product = dot3(matrix[...], power_high[:, :wide], power_low[:, :wide])
        power_high, power_low = split(product)
        powers[2 * (level - 1)][...] = power_high
        powers[2 * (level - 1) + 1][...] = power_low
        if level + 1 < levels:
            matrix[...] = product


def solve_kernel(steps, share, levels, parts, packed, *refs):
    partials, refs = refs[:parts], refs[parts:]
    (
        driving,
        earlier,
        inverse_high,
        inverse_low,
        coupling_high,
        coupling_low,
        first_high,
        first_low,
        *powers,
    ) = refs[: 8 + 2 * (levels - 1)]
    solved, sent, *following = refs[8 + 2 * (levels - 1) :]
    count, rows, _ = coupling_high.shape
    size = share * steps
    power_row = size + share * count if packed else size
    adjusted = driving[...].astype(F32)
    for partial in partials:
        adjusted = adjusted - unscaled(partial, size, power_row)
    row_of = lax.broadcasted_iota(jnp.int32, (size, 1), 0)
    padded = -(-share // SUBLANES) * SUBLANES
    if packed:
        known = partials[0][size:]
        for partial in partials[1:]:
            known = known + partial[size:]
    else:
        known = earlier[...]

    def back(lag):
        pieces = [
            known[item * count + count - lag : item * count + count - lag + 1]
            for item in range(share)
        ]
        pieces.append(jnp.zeros((padded - share, rows), F32))
        return jnp.concatenate(pieces, 0)

    for step in range(count):
        pull = None
        for lag in range(step + 1, count + 1):
            term = dot3(back(lag - step), coupling_high[lag - 1], coupling_low[lag - 1])
            pull = term if pull is None else pull + term
        for item in range(share):
            adjusted = adjusted - jnp.where(
                row_of == item * steps + step, pull[item : item + 1], 0.0
            )
    within = row_of % steps
    driven = dot3(adjusted, inverse_high[...], inverse_low[...])

    def delayed(value, delay):
        return jnp.where(within >= delay, pltpu.roll(value, delay, 0), 0.0)

    columns = [driven + delayed(dot3(driven, first_high[...], first_low[...]), 1)]
    if count > 1:
        columns.append(delayed(driven, 1))
    columns += [jnp.zeros_like(driven)] * (count - 2)
    total = jnp.concatenate(columns, 1)
    for level in range(1, levels):
        high, low = powers[2 * (level - 1)], powers[2 * (level - 1) + 1]
        wide = high.shape[1]
        total = total[:, :wide] + delayed(dot3(total, high[...], low[...]), 2**level)
    result = total[:, :rows]
    solved[...] = result
    sent[:size], power = scaled(result)
    sent[size:] = jnp.broadcast_to(power, (sent.shape[0] - size, rows))
    if following:
        rounded, state = following
        rounded[...] = result.astype(BF16)
        state[...] = jnp.zeros_like(state)
        for item in range(share):
            state[item * count : (item + 1) * count] = result[
                (item + 1) * steps - count : (item + 1) * steps
            ]


def spread_kernel(block, share, own, *refs):
    (*chunks, out, ready, sems) = refs
    groups, steps, loads, _ = ready.shape
    rows_of = ready.reshape(groups, steps * loads, LANES)
    steps -= 1
    sources = (len(chunks) + 1) if block == 0 else len(chunks)
    size = share * steps
    source = lax.axis_index("src")
    copies = []
    for group in range(groups):
        lanes = slice(group * LANES, (group + 1) * LANES)
        for index, chunk in enumerate([own, *chunks][:sources]):
            first = sender(source, index, sources) * share % loads
            value = chunk[:size, lanes]
            if index > 0:
                value = value * jnp.exp2(chunk[size : size + 1, lanes] - HEADROOM)
            for item in range(share):
                rows_of[group, pl.ds(first + item, steps, stride=loads), :] = value[
                    item * steps : (item + 1) * steps
                ]
        copies.append(
            pltpu.make_async_copy(
                ready.at[group, pl.ds(0, steps)],
                out.at[pl.ds(block * steps, steps), :, pl.ds(group * LANES, LANES)],
                sems.at[group],
            )
        )
        copies[-1].start()
    for copy in copies:
        copy.wait()


def landing(plane, sources):
    shares = sorted(range(sources), key=lambda z: (-abs(z - plane), z))
    if sources & (sources - 1) == 0:
        chips = sorted(range(sources), key=lambda e: (bin(e ^ plane).count("1"), e))
    else:
        chips = sorted(range(sources), key=lambda e: (abs(e - plane), e))
    where = [0] * sources
    for one, chip in zip(shares, chips):
        where[one] = chip
    return where


def local(incident, past_density, kernels, lag_offset, lag_counts, couplings, inverse):
    all_steps, loads, rows = incident.shape
    columns = past_density.shape[2]
    slots = kernels.shape[0]
    span = lag_offset.shape[2]
    steps = past_density.shape[0] - span
    blocks = all_steps // steps
    count = couplings.shape[0]
    levels = steps.bit_length() - 1
    ratio = columns // rows
    sources = lax.axis_size("src")
    targets = lax.axis_size("tgt")
    target = lax.axis_index("tgt")
    source = lax.axis_index("src")
    share = max(loads // sources, 1)
    size = share * steps
    groups = rows // LANES
    pad = -(-(share * count + 1) // SUBLANES) * SUBLANES

    table = [landing(plane, sources) for plane in range(sources)]

    def params(mebibytes):
        return pltpu.CompilerParams(vmem_limit_bytes=mebibytes * 2**20)

    def cost(work):
        return pl.CostEstimate(flops=work * 10**9, bytes_accessed=0, transcendentals=0)

    def trade(value, shift):
        pairs = [(i, partner(i, shift, sources)) for i in range(sources)]
        return lax.ppermute(value, "src", pairs)

    def trade_each(values):
        return [
            trade(value.astype(jnp.float16), k).astype(F32)
            for k, value in enumerate(values, 1)
        ]

    prepared = pl.pallas_call(
        functools.partial(prepare_kernel, levels),
        out_shape=[jax.ShapeDtypeStruct((rows, rows), BF16)] * 2
        + [jax.ShapeDtypeStruct((count, rows, rows), BF16)] * 2
        + [jax.ShapeDtypeStruct((rows, rows), BF16)] * 2
        + [jax.ShapeDtypeStruct((count * rows, count * rows), BF16)] * (2 * (levels - 2))
        + [jax.ShapeDtypeStruct((count * rows, rows), BF16)] * 2,
        in_specs=[VMEM, VMEM],
        out_specs=[VMEM] * (6 + 2 * (levels - 1)),
        scratch_shapes=[pltpu.VMEM((count * rows, count * rows), F32)],
        compiler_params=params(16),
        cost_estimate=cost(5),
        name="prepare",
    )(couplings, inverse)

    def solve(partials, driving, earlier, first, last):
        operands = [*partials, driving, earlier, *prepared]
        shapes = [
            jax.ShapeDtypeStruct((size, rows), F32),
            jax.ShapeDtypeStruct((size + SUBLANES, rows), F32),
        ]
        if not last:
            shapes.append(jax.ShapeDtypeStruct((size, rows), BF16))
            shapes.append(jax.ShapeDtypeStruct((pad, rows), F32))
        return pl.pallas_call(
            functools.partial(solve_kernel, steps, share, levels, len(partials), first),
            out_shape=shapes,
            in_specs=[VMEM] * len(operands),
            out_specs=[VMEM] * len(shapes),
            compiler_params=params(12),
            cost_estimate=cost(3),
            name="solve",
        )(*operands)

    def spread(block, before, own, chunks):
        last = [] if block == 0 else [before]
        return pl.pallas_call(
            functools.partial(spread_kernel, block, share),
            out_shape=jax.ShapeDtypeStruct((all_steps, loads, rows), F32),
            in_specs=[VMEM] * sources + [HBM] * len(last),
            out_specs=HBM,
            scratch_shapes=[
                pltpu.VMEM((groups, steps + 1, loads, LANES), F32),
                pltpu.SemaphoreType.DMA((groups,)),
            ],
            input_output_aliases={sources: 0} if last else {},
            compiler_params=params(8),
            name="spread",
        )(own, *chunks, *last)

    own_incident = lax.dynamic_slice_in_dim(incident, source * share % loads, share, 1)
    own_incident = own_incident.reshape(blocks, steps, share, rows)
    own_incident = own_incident.transpose(0, 2, 1, 3).reshape(blocks, size, rows)

    total_scratch = pltpu.VMEM((groups, (steps + 1) * loads, LANES), F32)
    history_scratch = pltpu.VMEM((span + steps, loads, columns), BF16)

    *partials, tail = pl.pallas_call(
        functools.partial(far_first_kernel, span, count, share, sources, ratio),
        out_shape=[jax.ShapeDtypeStruct((size + pad, rows), F32)] * sources
        + [jax.ShapeDtypeStruct((span, loads, columns), BF16)],
        in_specs=[SMEM, HBM, HBM, HBM],
        out_specs=[VMEM] * (sources + 1),
        scratch_shapes=[
            history_scratch,
            pltpu.VMEM(kernels.shape, BF16),
            total_scratch,
            pltpu.SMEM(lag_offset.shape, jnp.int32),
            pltpu.SemaphoreType.DMA((slots,)),
            pltpu.SemaphoreType.DMA,
            pltpu.SemaphoreType.DMA,
        ],
        compiler_params=params(53),
        cost_estimate=cost(2),
        name="far_first",
    )(lag_counts, lag_offset, past_density, kernels)

    state = jnp.zeros((pad, rows), F32)
    output = None
    for block in range(blocks):
        if block > 0:
            moves = [
                (
                    (one * ratio + part) * sources + z,
                    (table[one][z] * ratio + part) * sources + one,
                )
                for one in range(sources)
                for part in range(ratio)
                for z in range(sources)
            ]
            landed = lax.ppermute(rounded, ("tgt", "src"), moves)
            chunks = trade_each([sent] * (sources - 1))
            arrived = [landed]
            for k in range(1, sources):
                pairs = [
                    (e * ratio + part, partner(e, k, sources) * ratio + part)
                    for e in range(sources)
                    for part in range(ratio)
                ]
                arrived.append(lax.ppermute(landed, "tgt", pairs))
            swapped = []
            for turn in range(1, ratio):
                pairs = [
                    (e * ratio + part, e * ratio + (part + turn) % ratio)
                    for e in range(sources)
                    for part in range(ratio)
                ]
                swapped += [lax.ppermute(chunk, "tgt", pairs) for chunk in arrived]
            partials = pl.pallas_call(
                functools.partial(far_next_kernel, table, span, share, ratio),
                out_shape=[jax.ShapeDtypeStruct((size + SUBLANES, rows), F32)] * sources,
                in_specs=[SMEM, SMEM, VMEM, VMEM] + [VMEM] * (sources * ratio),
                out_specs=[VMEM] * sources,
                scratch_shapes=[
                    total_scratch,
                    pltpu.VMEM((columns // LANES, (steps + 1) * loads, LANES), F32),
                    history_scratch,
                ],
                compiler_params=params(12),
                cost_estimate=cost(3),
                name="far_next",
            )(lag_counts, lag_offset, tail, kernels, *arrived, *swapped)
            output = spread(block - 1, output, solved, chunks)
        received = [partials[0]] + trade_each(partials[1:])
        solved, sent, *following = solve(
            received, own_incident[block], state, block == 0, block + 1 == blocks
        )
        if following:
            rounded, state = following
    return spread(blocks - 1, output, solved, trade_each([sent] * (sources - 1)))


def solution(mesh):
    return jax.shard_map(
        local,
        mesh=mesh,
        in_specs=(
            P(None, None, "tgt"),
            P(None, None, "src"),
            P(None, "src", "tgt"),
            P("tgt", "src", None),
            P("tgt", "src"),
            P(None, "tgt", None),
            P("tgt", None),
        ),
        out_specs=P(None, None, "tgt"),
        check_vma=False,
    )
```

```python
import functools

import jax
import jax.numpy as jnp
from jax import lax
from jax.experimental import pallas as pl
from jax.experimental.pallas import tpu as pltpu
from jax.sharding import PartitionSpec as P

F32 = jnp.float32
BF16 = jnp.bfloat16
LANES = 128
SUBLANES = 8
VMEM = pl.BlockSpec(memory_space=pltpu.VMEM)
SMEM = pl.BlockSpec(memory_space=pltpu.SMEM)
HBM = pl.BlockSpec(memory_space=pltpu.HBM)


def partner(index, shift, count):
    if count & (count - 1) == 0:
        return index ^ shift
    return (index + shift) % count


def sender(index, shift, count):
    if count & (count - 1) == 0:
        return index ^ shift
    return (index - shift) % count


def split(value):
    high = value.astype(BF16)
    return high, (value - high.astype(F32)).astype(BF16)


def dot3(value, high, low):
    rows = value.shape[0]
    value_high, value_low = split(value)
    both = jnp.dot(
        jnp.concatenate([value_high, value_low], 0), high, preferred_element_type=F32
    )
    cross = jnp.dot(value_high, low, preferred_element_type=F32)
    return both[:rows] + (both[rows:] + cross)


HEADROOM = 13.0
SMALLEST = 2.0**-100


def scaled(chunk):
    largest = jnp.max(jnp.max(jnp.abs(chunk), axis=0, keepdims=True), axis=1, keepdims=True)
    power = jnp.floor(jnp.log2(jnp.maximum(largest, SMALLEST)))
    return chunk * jnp.exp2(HEADROOM - power), power


def unscaled(packed, size, row):
    return packed[:size] * jnp.exp2(packed[row : row + 1] - HEADROOM)


def start_slots(counts, kernels, kernel_buffer, sems):
    for slot in range(kernel_buffer.shape[0]):

        @pl.when(slot < counts[0, 0])
        def _():
            pltpu.make_async_copy(
                kernels.at[slot], kernel_buffer.at[slot], sems.at[slot]
            ).start()


def sum_slots(counts, offsets, history, kernels, total, span, arrived=None):
    steps = history.shape[0] - span
    loads, columns = history.shape[1:]
    count = counts[0, 0]
    total[...] = jnp.zeros_like(total)

    def window(slot):
        taken = history[pl.ds(span - offsets[0, 0, slot], steps)]
        return taken.reshape(steps * loads, columns)

    def add(first, together):
        if arrived is not None:
            for slot in range(together):
                arrived(first + slot)
        windows = jnp.concatenate([window(first + slot) for slot in range(together)], 1)
        matrix = kernels[pl.ds(first, together)].reshape(together * columns, -1)
        product = jnp.dot(windows, matrix, preferred_element_type=F32)
        for group in range(total.shape[0]):
            total[group, : steps * loads] += product[:, group * LANES : (group + 1) * LANES]

    done = 0
    together = 1 << (kernels.shape[0].bit_length() - 1)
    while together:
        rounds = (count - done) // together

        def step(index, carry, first=done, together=together):
            add(first + index * together, together)
            return carry

        lax.fori_loop(0, rounds, step, 0)
        done += rounds * together
        together //= 2


def write_chunks(total, outs, share, loads, row):
    groups, size, _ = total.shape
    steps = size // loads - 1
    source, sources = lax.axis_index("src"), len(outs)
    for index, out in enumerate(outs):
        first = partner(source, index, sources) * share % loads
        columns = [
            jnp.concatenate(
                [
                    total[group, pl.ds(first + item, steps, stride=loads), :]
                    for item in range(share)
                ],
                0,
            )
            for group in range(groups)
        ]
        chunk = jnp.concatenate(columns, 1)
        if index > 0:
            chunk, power = scaled(chunk)
        else:
            power = jnp.full((1, 1), HEADROOM, F32)
        out[: share * steps] = chunk
        out[row : row + 1] = jnp.broadcast_to(power, (1, groups * LANES))


def far_first_kernel(
    span, couplings, share, sources, ratio, counts, offsets, past, kernels, *refs
):
    (*outs, tail, history, kernel_buffer, total, scalars, sems, past_sem, scalar_sem) = refs
    fetched = pltpu.make_async_copy(past, history, past_sem)
    listed = pltpu.make_async_copy(offsets, scalars, scalar_sem)
    listed.start()
    fetched.start()
    start_slots(counts, kernels, kernel_buffer, sems)
    steps = history.shape[0] - span
    loads = history.shape[1]
    groups = total.shape[0]
    rows = groups * LANES
    size = share * steps
    listed.wait()
    fetched.wait()
    tail[...] = history[steps:]

    def arrived(slot):
        pltpu.make_async_copy(
            kernels.at[slot], kernel_buffer.at[slot], sems.at[slot]
        ).wait()

    sum_slots(counts, scalars, history, kernel_buffer, total, span, arrived)
    for out in outs:
        out[size:] = jnp.zeros_like(out[size:])
    write_chunks(total, outs, share, loads, size + share * couplings)
    target, source = lax.axis_index("tgt"), lax.axis_index("src")
    holds = source == target // ratio
    at = pl.multiple_of(target % ratio * rows, LANES)
    recent = history[history.shape[0] - couplings :, :, pl.ds(at, rows)].astype(F32)
    recent = jnp.where(holds, recent, jnp.zeros_like(recent)).reshape(couplings * loads, rows)
    for group in range(groups):
        total[group, : couplings * loads] = recent[:, group * LANES : (group + 1) * LANES]
    for index, out in enumerate(outs):
        first = partner(source, index, sources) * share % loads
        for item in range(share):
            for step in range(couplings):
                row = size + item * couplings + step
                for group in range(groups):
                    out[row : row + 1, group * LANES : (group + 1) * LANES] = total[
                        group, pl.ds(step * loads + first + item, 1), :
                    ]


def far_next_kernel(table, span, share, ratio, counts, offsets, tail, kernels, *refs):
    sources = len(table)
    arrived, refs = refs[: sources * ratio], refs[sources * ratio :]
    (*outs, total, strided, history) = refs
    steps = history.shape[0] - span
    loads, columns = history.shape[1:]
    groups = total.shape[0]
    history[:span] = tail[...]
    target, source = lax.axis_index("tgt"), lax.axis_index("src")
    chip, own = target // ratio, lax.rem(target, ratio)
    for index in range(sources):
        first = 0
        for plane in range(sources):
            for one in range(sources):
                here = partner(table[plane][one], index, sources)
                first = jnp.where(
                    (source == plane) & (chip == here), one * share % loads, first
                )
        for turn in range(ratio):
            chunk = arrived[turn * sources + index]
            part = lax.rem(own + ratio - turn, ratio)
            for item in range(share):
                for group in range(groups):
                    strided[
                        part * groups + group,
                        pl.ds(first + item, steps, stride=loads),
                        :,
                    ] = chunk[
                        item * steps : (item + 1) * steps, group * LANES : (group + 1) * LANES
                    ].astype(F32)
    for group in range(columns // LANES):
        history[span:, :, group * LANES : (group + 1) * LANES] = (
            strided[group, : steps * loads].reshape(steps, loads, LANES).astype(BF16)
        )
    sum_slots(counts, offsets, history, kernels, total, span)
    write_chunks(total, outs, share, loads, share * steps)


def prepare_kernel(levels, couplings, inverse, *refs):
    (
        inverse_high,
        inverse_low,
        coupling_high,
        coupling_low,
        first_high,
        first_low,
        *powers,
        matrix,
    ) = refs
    count, rows, _ = couplings.shape
    high, low = split(inverse[...])
    inverse_high[...] = high
    inverse_low[...] = low
    matrix[...] = jnp.zeros_like(matrix)
    identity = (
        lax.broadcasted_iota(jnp.int32, (rows, rows), 0)
        == lax.broadcasted_iota(jnp.int32, (rows, rows), 1)
    ).astype(F32)
    for lag in range(count):
        coupling_high[lag], coupling_low[lag] = split(couplings[lag])
        matrix[lag * rows : (lag + 1) * rows, :rows] = -dot3(couplings[lag], high, low)
        if lag + 1 < count:
            matrix[
                lag * rows : (lag + 1) * rows, (lag + 1) * rows : (lag + 2) * rows
            ] = identity
    first_high[...], first_low[...] = split(matrix[:rows, :rows])
    power_high, power_low = split(matrix[...])
    for level in range(1, levels):
        wide = powers[2 * (level - 1)].shape[1]
        if level == 1 and wide == count * rows:
            column = matrix[:, :rows]
            product = dot3(column, first_high[...], first_low[...])
            product += jnp.concatenate([column[rows:], jnp.zeros((rows, rows), F32)], 0)
            product = jnp.concatenate([product, matrix[:, : wide - rows]], 1)
        else:
            product = dot3(matrix[...], power_high[:, :wide], power_low[:, :wide])
        power_high, power_low = split(product)
        powers[2 * (level - 1)][...] = power_high
        powers[2 * (level - 1) + 1][...] = power_low
        if level + 1 < levels:
            matrix[...] = product


def solve_kernel(steps, share, levels, parts, packed, *refs):
    partials, refs = refs[:parts], refs[parts:]
    (
        driving,
        earlier,
        inverse_high,
        inverse_low,
        coupling_high,
        coupling_low,
        first_high,
        first_low,
        *powers,
    ) = refs[: 8 + 2 * (levels - 1)]
    solved, sent, *following = refs[8 + 2 * (levels - 1) :]
    count, rows, _ = coupling_high.shape
    size = share * steps
    power_row = size + share * count if packed else size
    adjusted = driving[...].astype(F32)
    for partial in partials:
        adjusted = adjusted - unscaled(partial, size, power_row)
    row_of = lax.broadcasted_iota(jnp.int32, (size, 1), 0)
    padded = -(-share // SUBLANES) * SUBLANES
    if packed:
        known = partials[0][size:]
        for partial in partials[1:]:
            known = known + partial[size:]
    else:
        known = earlier[...]

    def back(lag):
        pieces = [
            known[item * count + count - lag : item * count + count - lag + 1]
            for item in range(share)
        ]
        pieces.append(jnp.zeros((padded - share, rows), F32))
        return jnp.concatenate(pieces, 0)

    nothing = jnp.zeros((padded, rows), F32)
    reached = [
        jnp.concatenate(
            [back(lag - step) if lag > step else nothing for lag in range(1, count + 1)], 1
        )
        for step in range(count)
    ]
    pull = dot3(
        jnp.concatenate(reached, 0),
        coupling_high[...].reshape(count * rows, rows),
        coupling_low[...].reshape(count * rows, rows),
    )
    for step in range(count):
        for item in range(share):
            at = step * padded + item
            adjusted = adjusted - jnp.where(
                row_of == item * steps + step, pull[at : at + 1], 0.0
            )
    within = row_of % steps
    driven = dot3(adjusted, inverse_high[...], inverse_low[...])

    def delayed(value, delay):
        return jnp.where(within >= delay, pltpu.roll(value, delay, 0), 0.0)

    columns = [driven + delayed(dot3(driven, first_high[...], first_low[...]), 1)]
    if count > 1:
        columns.append(delayed(driven, 1))
    columns += [jnp.zeros_like(driven)] * (count - 2)
    total = jnp.concatenate(columns, 1)
    for level in range(1, levels):
        high, low = powers[2 * (level - 1)], powers[2 * (level - 1) + 1]
        wide = high.shape[1]
        total = total[:, :wide] + delayed(dot3(total, high[...], low[...]), 2**level)
    result = total[:, :rows]
    solved[...] = result
    sent[:size], power = scaled(result)
    sent[size:] = jnp.broadcast_to(power, (sent.shape[0] - size, rows))
    if following:
        rounded, state = following
        rounded[...] = result.astype(BF16)
        state[...] = jnp.zeros_like(state)
        for item in range(share):
            state[item * count : (item + 1) * count] = result[
                (item + 1) * steps - count : (item + 1) * steps
            ]


def spread_kernel(block, share, own, *refs):
    (*chunks, out, ready, sems) = refs
    groups, steps, loads, _ = ready.shape
    rows_of = ready.reshape(groups, steps * loads, LANES)
    steps -= 1
    sources = (len(chunks) + 1) if block == 0 else len(chunks)
    size = share * steps
    source = lax.axis_index("src")
    copies = []
    for group in range(groups):
        lanes = slice(group * LANES, (group + 1) * LANES)
        for index, chunk in enumerate([own, *chunks][:sources]):
            first = sender(source, index, sources) * share % loads
            value = chunk[:size, lanes]
            if index > 0:
                value = value * jnp.exp2(chunk[size : size + 1, lanes] - HEADROOM)
            for item in range(share):
                rows_of[group, pl.ds(first + item, steps, stride=loads), :] = value[
                    item * steps : (item + 1) * steps
                ]
        copies.append(
            pltpu.make_async_copy(
                ready.at[group, pl.ds(0, steps)],
                out.at[pl.ds(block * steps, steps), :, pl.ds(group * LANES, LANES)],
                sems.at[group],
            )
        )
        copies[-1].start()
    for copy in copies:
        copy.wait()


def landing(plane, sources):
    shares = sorted(range(sources), key=lambda z: (-abs(z - plane), z))
    if sources & (sources - 1) == 0:
        chips = sorted(range(sources), key=lambda e: (bin(e ^ plane).count("1"), e))
    else:
        chips = sorted(range(sources), key=lambda e: (abs(e - plane), e))
    where = [0] * sources
    for one, chip in zip(shares, chips):
        where[one] = chip
    return where


def local(incident, past_density, kernels, lag_offset, lag_counts, couplings, inverse):
    all_steps, loads, rows = incident.shape
    columns = past_density.shape[2]
    slots = kernels.shape[0]
    span = lag_offset.shape[2]
    steps = past_density.shape[0] - span
    blocks = all_steps // steps
    count = couplings.shape[0]
    levels = steps.bit_length() - 1
    ratio = columns // rows
    sources = lax.axis_size("src")
    targets = lax.axis_size("tgt")
    target = lax.axis_index("tgt")
    source = lax.axis_index("src")
    share = max(loads // sources, 1)
    size = share * steps
    groups = rows // LANES
    pad = -(-(share * count + 1) // SUBLANES) * SUBLANES

    table = [landing(plane, sources) for plane in range(sources)]

    def params(mebibytes):
        return pltpu.CompilerParams(vmem_limit_bytes=mebibytes * 2**20)

    def cost(work):
        return pl.CostEstimate(flops=work * 10**9, bytes_accessed=0, transcendentals=0)

    def trade(value, shift):
        pairs = [(i, partner(i, shift, sources)) for i in range(sources)]
        return lax.ppermute(value, "src", pairs)

    def trade_each(values):
        return [
            trade(value.astype(jnp.float16), k).astype(F32)
            for k, value in enumerate(values, 1)
        ]

    prepared = pl.pallas_call(
        functools.partial(prepare_kernel, levels),
        out_shape=[jax.ShapeDtypeStruct((rows, rows), BF16)] * 2
        + [jax.ShapeDtypeStruct((count, rows, rows), BF16)] * 2
        + [jax.ShapeDtypeStruct((rows, rows), BF16)] * 2
        + [jax.ShapeDtypeStruct((count * rows, count * rows), BF16)] * (2 * (levels - 2))
        + [jax.ShapeDtypeStruct((count * rows, rows), BF16)] * 2,
        in_specs=[VMEM, VMEM],
        out_specs=[VMEM] * (6 + 2 * (levels - 1)),
        scratch_shapes=[pltpu.VMEM((count * rows, count * rows), F32)],
        compiler_params=params(16),
        cost_estimate=cost(5),
        name="prepare",
    )(couplings, inverse)

    def solve(partials, driving, earlier, first, last):
        operands = [*partials, driving, earlier, *prepared]
        shapes = [
            jax.ShapeDtypeStruct((size, rows), F32),
            jax.ShapeDtypeStruct((size + SUBLANES, rows), F32),
        ]
        if not last:
            shapes.append(jax.ShapeDtypeStruct((size, rows), BF16))
            shapes.append(jax.ShapeDtypeStruct((pad, rows), F32))
        return pl.pallas_call(
            functools.partial(solve_kernel, steps, share, levels, len(partials), first),
            out_shape=shapes,
            in_specs=[VMEM] * len(operands),
            out_specs=[VMEM] * len(shapes),
            compiler_params=params(12),
            cost_estimate=cost(3),
            name="solve",
        )(*operands)

    def spread(block, before, own, chunks):
        last = [] if block == 0 else [before]
        return pl.pallas_call(
            functools.partial(spread_kernel, block, share),
            out_shape=jax.ShapeDtypeStruct((all_steps, loads, rows), F32),
            in_specs=[VMEM] * sources + [HBM] * len(last),
            out_specs=HBM,
            scratch_shapes=[
                pltpu.VMEM((groups, steps + 1, loads, LANES), F32),
                pltpu.SemaphoreType.DMA((groups,)),
            ],
            input_output_aliases={sources: 0} if last else {},
            compiler_params=params(8),
            name="spread",
        )(own, *chunks, *last)

    own_incident = lax.dynamic_slice_in_dim(incident, source * share % loads, share, 1)
    own_incident = own_incident.reshape(blocks, steps, share, rows)
    own_incident = own_incident.transpose(0, 2, 1, 3).reshape(blocks, size, rows)

    total_scratch = pltpu.VMEM((groups, (steps + 1) * loads, LANES), F32)
    history_scratch = pltpu.VMEM((span + steps, loads, columns), BF16)

    *partials, tail = pl.pallas_call(
        functools.partial(far_first_kernel, span, count, share, sources, ratio),
        out_shape=[jax.ShapeDtypeStruct((size + pad, rows), F32)] * sources
        + [jax.ShapeDtypeStruct((span, loads, columns), BF16)],
        in_specs=[SMEM, HBM, HBM, HBM],
        out_specs=[VMEM] * (sources + 1),
        scratch_shapes=[
            history_scratch,
            pltpu.VMEM(kernels.shape, BF16),
            total_scratch,
            pltpu.SMEM(lag_offset.shape, jnp.int32),
            pltpu.SemaphoreType.DMA((slots,)),
            pltpu.SemaphoreType.DMA,
            pltpu.SemaphoreType.DMA,
        ],
        compiler_params=params(53),
        cost_estimate=cost(2),
        name="far_first",
    )(lag_counts, lag_offset, past_density, kernels)

    state = jnp.zeros((pad, rows), F32)
    output = None
    for block in range(blocks):
        if block > 0:
            moves = [
                (
                    (one * ratio + part) * sources + z,
                    (table[one][z] * ratio + part) * sources + one,
                )
                for one in range(sources)
                for part in range(ratio)
                for z in range(sources)
            ]
            landed = lax.ppermute(rounded, ("tgt", "src"), moves)
            chunks = trade_each([sent] * (sources - 1))
            arrived = [landed]
            for k in range(1, sources):
                pairs = [
                    (e * ratio + part, partner(e, k, sources) * ratio + part)
                    for e in range(sources)
                    for part in range(ratio)
                ]
                arrived.append(lax.ppermute(landed, "tgt", pairs))
            swapped = []
            for turn in range(1, ratio):
                pairs = [
                    (e * ratio + part, e * ratio + (part + turn) % ratio)
                    for e in range(sources)
                    for part in range(ratio)
                ]
                swapped += [lax.ppermute(chunk, "tgt", pairs) for chunk in arrived]
            partials = pl.pallas_call(
                functools.partial(far_next_kernel, table, span, share, ratio),
                out_shape=[jax.ShapeDtypeStruct((size + SUBLANES, rows), F32)] * sources,
                in_specs=[SMEM, SMEM, VMEM, VMEM] + [VMEM] * (sources * ratio),
                out_specs=[VMEM] * sources,
                scratch_shapes=[
                    total_scratch,
                    pltpu.VMEM((columns // LANES, (steps + 1) * loads, LANES), F32),
                    history_scratch,
                ],
                compiler_params=params(12),
                cost_estimate=cost(3),
                name="far_next",
            )(lag_counts, lag_offset, tail, kernels, *arrived, *swapped)
            output = spread(block - 1, output, solved, chunks)
        received = [partials[0]] + trade_each(partials[1:])
        solved, sent, *following = solve(
            received, own_incident[block], state, block == 0, block + 1 == blocks
        )
        if following:
            rounded, state = following
    return spread(blocks - 1, output, solved, trade_each([sent] * (sources - 1)))


def solution(mesh):
    return jax.shard_map(
        local,
        mesh=mesh,
        in_specs=(
            P(None, None, "tgt"),
            P(None, None, "src"),
            P(None, "src", "tgt"),
            P("tgt", "src", None),
            P("tgt", "src"),
            P(None, "tgt", None),
            P("tgt", None),
        ),
        out_specs=P(None, None, "tgt"),
        check_vma=False,
    )
```

```python
import functools

import jax
import jax.numpy as jnp
from jax import lax
from jax.experimental import pallas as pl
from jax.experimental.pallas import tpu as pltpu
from jax.sharding import PartitionSpec as P

F32 = jnp.float32
BF16 = jnp.bfloat16
LANES = 128
SUBLANES = 8
VMEM = pl.BlockSpec(memory_space=pltpu.VMEM)
SMEM = pl.BlockSpec(memory_space=pltpu.SMEM)
HBM = pl.BlockSpec(memory_space=pltpu.HBM)


def partner(index, shift, count):
    if count & (count - 1) == 0:
        return index ^ shift
    return (index + shift) % count


def sender(index, shift, count):
    if count & (count - 1) == 0:
        return index ^ shift
    return (index - shift) % count


def split(value):
    high = value.astype(BF16)
    return high, (value - high.astype(F32)).astype(BF16)


def dot3(value, high, low):
    rows = value.shape[0]
    value_high, value_low = split(value)
    both = jnp.dot(
        jnp.concatenate([value_high, value_low], 0), high, preferred_element_type=F32
    )
    cross = jnp.dot(value_high, low, preferred_element_type=F32)
    return both[:rows] + (both[rows:] + cross)


HEADROOM = 13.0
SMALLEST = 2.0**-100


def scaled(chunk):
    largest = jnp.max(jnp.max(jnp.abs(chunk), axis=0, keepdims=True), axis=1, keepdims=True)
    power = jnp.floor(jnp.log2(jnp.maximum(largest, SMALLEST)))
    return chunk * jnp.exp2(HEADROOM - power), power


def unscaled(packed, size, row):
    return packed[:size] * jnp.exp2(packed[row : row + 1] - HEADROOM)


def start_slots(counts, kernels, kernel_buffer, sems):
    for slot in range(kernel_buffer.shape[0]):

        @pl.when(slot < counts[0, 0])
        def _():
            pltpu.make_async_copy(
                kernels.at[slot], kernel_buffer.at[slot], sems.at[slot]
            ).start()


def sum_slots(counts, offsets, history, kernels, total, span, arrived=None):
    steps = history.shape[0] - span
    loads, columns = history.shape[1:]
    count = counts[0, 0]
    total[...] = jnp.zeros_like(total)

    def window(slot):
        taken = history[pl.ds(span - offsets[0, 0, slot], steps)]
        return taken.reshape(steps * loads, columns)

    def add(first, together):
        if arrived is not None:
            for slot in range(together):
                arrived(first + slot)
        windows = jnp.concatenate([window(first + slot) for slot in range(together)], 1)
        matrix = kernels[pl.ds(first, together)].reshape(together * columns, -1)
        product = jnp.dot(windows, matrix, preferred_element_type=F32)
        for group in range(total.shape[0]):
            total[group, : steps * loads] += product[:, group * LANES : (group + 1) * LANES]

    done = 0
    together = 1 << (kernels.shape[0].bit_length() - 1)
    while together:
        rounds = (count - done) // together

        def step(index, carry, first=done, together=together):
            add(first + index * together, together)
            return carry

        lax.fori_loop(0, rounds, step, 0)
        done += rounds * together
        together //= 2


def write_chunks(total, outs, share, loads, row):
    groups, size, _ = total.shape
    steps = size // loads - 1
    source, sources = lax.axis_index("src"), len(outs)
    for index, out in enumerate(outs):
        first = partner(source, index, sources) * share % loads
        columns = [
            jnp.concatenate(
                [
                    total[group, pl.ds(first + item, steps, stride=loads), :]
                    for item in range(share)
                ],
                0,
            )
            for group in range(groups)
        ]
        chunk = jnp.concatenate(columns, 1)
        if index > 0:
            chunk, power = scaled(chunk)
        else:
            power = jnp.full((1, 1), HEADROOM, F32)
        out[: share * steps] = chunk
        out[row : row + 1] = jnp.broadcast_to(power, (1, groups * LANES))


def far_first_kernel(
    span, couplings, share, sources, ratio, counts, offsets, past, kernels, *refs
):
    (*outs, tail, history, kernel_buffer, total, scalars, sems, past_sem, scalar_sem) = refs
    fetched = pltpu.make_async_copy(past, history, past_sem)
    listed = pltpu.make_async_copy(offsets, scalars, scalar_sem)
    listed.start()
    fetched.start()
    start_slots(counts, kernels, kernel_buffer, sems)
    steps = history.shape[0] - span
    loads = history.shape[1]
    groups = total.shape[0]
    rows = groups * LANES
    size = share * steps
    listed.wait()
    fetched.wait()
    tail[...] = history[steps:]

    for out in outs:
        out[size:] = jnp.zeros_like(out[size:])
    target, source = lax.axis_index("tgt"), lax.axis_index("src")
    holds = source == target // ratio
    at = pl.multiple_of(target % ratio * rows, LANES)
    recent = history[history.shape[0] - couplings :, :, pl.ds(at, rows)].astype(F32)
    recent = jnp.where(holds, recent, jnp.zeros_like(recent)).reshape(couplings * loads, rows)
    for group in range(groups):
        total[group, : couplings * loads] = recent[:, group * LANES : (group + 1) * LANES]
    for index, out in enumerate(outs):
        first = partner(source, index, sources) * share % loads
        for item in range(share):
            for step in range(couplings):
                row = size + item * couplings + step
                for group in range(groups):
                    out[row : row + 1, group * LANES : (group + 1) * LANES] = total[
                        group, pl.ds(step * loads + first + item, 1), :
                    ]

    def arrived(slot):
        pltpu.make_async_copy(
            kernels.at[slot], kernel_buffer.at[slot], sems.at[slot]
        ).wait()

    sum_slots(counts, scalars, history, kernel_buffer, total, span, arrived)
    write_chunks(total, outs, share, loads, size + share * couplings)


def far_next_kernel(table, span, share, ratio, counts, offsets, tail, kernels, *refs):
    sources = len(table)
    arrived, refs = refs[: sources * ratio], refs[sources * ratio :]
    (*outs, total, strided, history) = refs
    steps = history.shape[0] - span
    loads, columns = history.shape[1:]
    groups = total.shape[0]
    history[:span] = tail[...]
    target, source = lax.axis_index("tgt"), lax.axis_index("src")
    chip, own = target // ratio, lax.rem(target, ratio)
    for index in range(sources):
        first = 0
        for plane in range(sources):
            for one in range(sources):
                here = partner(table[plane][one], index, sources)
                first = jnp.where(
                    (source == plane) & (chip == here), one * share % loads, first
                )
        for turn in range(ratio):
            chunk = arrived[turn * sources + index]
            part = lax.rem(own + ratio - turn, ratio)
            for item in range(share):
                for group in range(groups):
                    strided[
                        part * groups + group,
                        pl.ds(first + item, steps, stride=loads),
                        :,
                    ] = chunk[
                        item * steps : (item + 1) * steps, group * LANES : (group + 1) * LANES
                    ].astype(F32)
    for group in range(columns // LANES):
        history[span:, :, group * LANES : (group + 1) * LANES] = (
            strided[group, : steps * loads].reshape(steps, loads, LANES).astype(BF16)
        )
    sum_slots(counts, offsets, history, kernels, total, span)
    write_chunks(total, outs, share, loads, share * steps)


def prepare_kernel(levels, couplings, inverse, *refs):
    (
        inverse_high,
        inverse_low,
        coupling_high,
        coupling_low,
        first_high,
        first_low,
        *powers,
        matrix,
    ) = refs
    count, rows, _ = couplings.shape
    high, low = split(inverse[...])
    inverse_high[...] = high
    inverse_low[...] = low
    matrix[...] = jnp.zeros_like(matrix)
    identity = (
        lax.broadcasted_iota(jnp.int32, (rows, rows), 0)
        == lax.broadcasted_iota(jnp.int32, (rows, rows), 1)
    ).astype(F32)
    for lag in range(count):
        coupling_high[lag], coupling_low[lag] = split(couplings[lag])
        matrix[lag * rows : (lag + 1) * rows, :rows] = -dot3(couplings[lag], high, low)
        if lag + 1 < count:
            matrix[
                lag * rows : (lag + 1) * rows, (lag + 1) * rows : (lag + 2) * rows
            ] = identity
    first_high[...], first_low[...] = split(matrix[:rows, :rows])
    power_high, power_low = split(matrix[...])
    for level in range(1, levels):
        wide = powers[2 * (level - 1)].shape[1]
        if level == 1 and wide == count * rows:
            column = matrix[:, :rows]
            product = dot3(column, first_high[...], first_low[...])
            product += jnp.concatenate([column[rows:], jnp.zeros((rows, rows), F32)], 0)
            product = jnp.concatenate([product, matrix[:, : wide - rows]], 1)
        else:
            product = dot3(matrix[...], power_high[:, :wide], power_low[:, :wide])
        power_high, power_low = split(product)
        powers[2 * (level - 1)][...] = power_high
        powers[2 * (level - 1) + 1][...] = power_low
        if level + 1 < levels:
            matrix[...] = product


def solve_kernel(steps, share, levels, parts, packed, *refs):
    partials, refs = refs[:parts], refs[parts:]
    (
        driving,
        earlier,
        inverse_high,
        inverse_low,
        coupling_high,
        coupling_low,
        first_high,
        first_low,
        *powers,
    ) = refs[: 8 + 2 * (levels - 1)]
    solved, sent, *following = refs[8 + 2 * (levels - 1) :]
    count, rows, _ = coupling_high.shape
    size = share * steps
    power_row = size + share * count if packed else size
    adjusted = driving[...].astype(F32)
    for partial in partials:
        adjusted = adjusted - unscaled(partial, size, power_row)
    row_of = lax.broadcasted_iota(jnp.int32, (size, 1), 0)
    padded = -(-share // SUBLANES) * SUBLANES
    if packed:
        known = partials[0][size:]
        for partial in partials[1:]:
            known = known + partial[size:]
    else:
        known = earlier[...]

    def back(lag):
        pieces = [
            known[item * count + count - lag : item * count + count - lag + 1]
            for item in range(share)
        ]
        pieces.append(jnp.zeros((padded - share, rows), F32))
        return jnp.concatenate(pieces, 0)

    for step in range(count):
        pull = None
        for lag in range(step + 1, count + 1):
            term = dot3(back(lag - step), coupling_high[lag - 1], coupling_low[lag - 1])
            pull = term if pull is None else pull + term
        for item in range(share):
            adjusted = adjusted - jnp.where(
                row_of == item * steps + step, pull[item : item + 1], 0.0
            )
    within = row_of % steps
    driven = dot3(adjusted, inverse_high[...], inverse_low[...])

    def delayed(value, delay):
        return jnp.where(within >= delay, pltpu.roll(value, delay, 0), 0.0)

    columns = [driven + delayed(dot3(driven, first_high[...], first_low[...]), 1)]
    if count > 1:
        columns.append(delayed(driven, 1))
    columns += [jnp.zeros_like(driven)] * (count - 2)
    total = jnp.concatenate(columns, 1)
    for level in range(1, levels):
        high, low = powers[2 * (level - 1)], powers[2 * (level - 1) + 1]
        wide = high.shape[1]
        total = total[:, :wide] + delayed(dot3(total, high[...], low[...]), 2**level)
    result = total[:, :rows]
    solved[...] = result
    sent[:size], power = scaled(result)
    sent[size:] = jnp.broadcast_to(power, (sent.shape[0] - size, rows))
    if following:
        rounded, state = following
        rounded[...] = result.astype(BF16)
        state[...] = jnp.zeros_like(state)
        for item in range(share):
            state[item * count : (item + 1) * count] = result[
                (item + 1) * steps - count : (item + 1) * steps
            ]


def spread_kernel(block, share, own, *refs):
    (*chunks, out, ready, sems) = refs
    groups, steps, loads, _ = ready.shape
    rows_of = ready.reshape(groups, steps * loads, LANES)
    steps -= 1
    sources = (len(chunks) + 1) if block == 0 else len(chunks)
    size = share * steps
    source = lax.axis_index("src")
    copies = []
    for group in range(groups):
        lanes = slice(group * LANES, (group + 1) * LANES)
        for index, chunk in enumerate([own, *chunks][:sources]):
            first = sender(source, index, sources) * share % loads
            value = chunk[:size, lanes]
            if index > 0:
                value = value * jnp.exp2(chunk[size : size + 1, lanes] - HEADROOM)
            for item in range(share):
                rows_of[group, pl.ds(first + item, steps, stride=loads), :] = value[
                    item * steps : (item + 1) * steps
                ]
        copies.append(
            pltpu.make_async_copy(
                ready.at[group, pl.ds(0, steps)],
                out.at[pl.ds(block * steps, steps), :, pl.ds(group * LANES, LANES)],
                sems.at[group],
            )
        )
        copies[-1].start()
    for copy in copies:
        copy.wait()


def landing(plane, sources):
    shares = sorted(range(sources), key=lambda z: (-abs(z - plane), z))
    if sources & (sources - 1) == 0:
        chips = sorted(range(sources), key=lambda e: (bin(e ^ plane).count("1"), e))
    else:
        chips = sorted(range(sources), key=lambda e: (abs(e - plane), e))
    where = [0] * sources
    for one, chip in zip(shares, chips):
        where[one] = chip
    return where


def local(incident, past_density, kernels, lag_offset, lag_counts, couplings, inverse):
    all_steps, loads, rows = incident.shape
    columns = past_density.shape[2]
    slots = kernels.shape[0]
    span = lag_offset.shape[2]
    steps = past_density.shape[0] - span
    blocks = all_steps // steps
    count = couplings.shape[0]
    levels = steps.bit_length() - 1
    ratio = columns // rows
    sources = lax.axis_size("src")
    targets = lax.axis_size("tgt")
    target = lax.axis_index("tgt")
    source = lax.axis_index("src")
    share = max(loads // sources, 1)
    size = share * steps
    groups = rows // LANES
    pad = -(-(share * count + 1) // SUBLANES) * SUBLANES

    table = [landing(plane, sources) for plane in range(sources)]

    def params(mebibytes):
        return pltpu.CompilerParams(vmem_limit_bytes=mebibytes * 2**20)

    def cost(work):
        return pl.CostEstimate(flops=work * 10**9, bytes_accessed=0, transcendentals=0)

    def trade(value, shift):
        pairs = [(i, partner(i, shift, sources)) for i in range(sources)]
        return lax.ppermute(value, "src", pairs)

    def trade_each(values):
        return [
            trade(value.astype(jnp.float16), k).astype(F32)
            for k, value in enumerate(values, 1)
        ]

    prepared = pl.pallas_call(
        functools.partial(prepare_kernel, levels),
        out_shape=[jax.ShapeDtypeStruct((rows, rows), BF16)] * 2
        + [jax.ShapeDtypeStruct((count, rows, rows), BF16)] * 2
        + [jax.ShapeDtypeStruct((rows, rows), BF16)] * 2
        + [jax.ShapeDtypeStruct((count * rows, count * rows), BF16)] * (2 * (levels - 2))
        + [jax.ShapeDtypeStruct((count * rows, rows), BF16)] * 2,
        in_specs=[VMEM, VMEM],
        out_specs=[VMEM] * (6 + 2 * (levels - 1)),
        scratch_shapes=[pltpu.VMEM((count * rows, count * rows), F32)],
        compiler_params=params(16),
        cost_estimate=cost(5),
        name="prepare",
    )(couplings, inverse)

    def solve(partials, driving, earlier, first, last):
        operands = [*partials, driving, earlier, *prepared]
        shapes = [
            jax.ShapeDtypeStruct((size, rows), F32),
            jax.ShapeDtypeStruct((size + SUBLANES, rows), F32),
        ]
        if not last:
            shapes.append(jax.ShapeDtypeStruct((size, rows), BF16))
            shapes.append(jax.ShapeDtypeStruct((pad, rows), F32))
        return pl.pallas_call(
            functools.partial(solve_kernel, steps, share, levels, len(partials), first),
            out_shape=shapes,
            in_specs=[VMEM] * len(operands),
            out_specs=[VMEM] * len(shapes),
            compiler_params=params(12),
            cost_estimate=cost(3),
            name="solve",
        )(*operands)

    def spread(block, before, own, chunks):
        last = [] if block == 0 else [before]
        return pl.pallas_call(
            functools.partial(spread_kernel, block, share),
            out_shape=jax.ShapeDtypeStruct((all_steps, loads, rows), F32),
            in_specs=[VMEM] * sources + [HBM] * len(last),
            out_specs=HBM,
            scratch_shapes=[
                pltpu.VMEM((groups, steps + 1, loads, LANES), F32),
                pltpu.SemaphoreType.DMA((groups,)),
            ],
            input_output_aliases={sources: 0} if last else {},
            compiler_params=params(8),
            name="spread",
        )(own, *chunks, *last)

    own_incident = lax.dynamic_slice_in_dim(incident, source * share % loads, share, 1)
    own_incident = own_incident.reshape(blocks, steps, share, rows)
    own_incident = own_incident.transpose(0, 2, 1, 3).reshape(blocks, size, rows)

    total_scratch = pltpu.VMEM((groups, (steps + 1) * loads, LANES), F32)
    history_scratch = pltpu.VMEM((span + steps, loads, columns), BF16)

    *partials, tail = pl.pallas_call(
        functools.partial(far_first_kernel, span, count, share, sources, ratio),
        out_shape=[jax.ShapeDtypeStruct((size + pad, rows), F32)] * sources
        + [jax.ShapeDtypeStruct((span, loads, columns), BF16)],
        in_specs=[SMEM, HBM, HBM, HBM],
        out_specs=[VMEM] * (sources + 1),
        scratch_shapes=[
            history_scratch,
            pltpu.VMEM(kernels.shape, BF16),
            total_scratch,
            pltpu.SMEM(lag_offset.shape, jnp.int32),
            pltpu.SemaphoreType.DMA((slots,)),
            pltpu.SemaphoreType.DMA,
            pltpu.SemaphoreType.DMA,
        ],
        compiler_params=params(53),
        cost_estimate=cost(2),
        name="far_first",
    )(lag_counts, lag_offset, past_density, kernels)

    state = jnp.zeros((pad, rows), F32)
    output = None
    for block in range(blocks):
        if block > 0:
            moves = [
                (
                    (one * ratio + part) * sources + z,
                    (table[one][z] * ratio + part) * sources + one,
                )
                for one in range(sources)
                for part in range(ratio)
                for z in range(sources)
            ]
            landed = lax.ppermute(rounded, ("tgt", "src"), moves)
            chunks = trade_each([sent] * (sources - 1))
            arrived = [landed]
            for k in range(1, sources):
                pairs = [
                    (e * ratio + part, partner(e, k, sources) * ratio + part)
                    for e in range(sources)
                    for part in range(ratio)
                ]
                arrived.append(lax.ppermute(landed, "tgt", pairs))
            swapped = []
            for turn in range(1, ratio):
                pairs = [
                    (e * ratio + part, e * ratio + (part + turn) % ratio)
                    for e in range(sources)
                    for part in range(ratio)
                ]
                swapped += [lax.ppermute(chunk, "tgt", pairs) for chunk in arrived]
            partials = pl.pallas_call(
                functools.partial(far_next_kernel, table, span, share, ratio),
                out_shape=[jax.ShapeDtypeStruct((size + SUBLANES, rows), F32)] * sources,
                in_specs=[SMEM, SMEM, VMEM, VMEM] + [VMEM] * (sources * ratio),
                out_specs=[VMEM] * sources,
                scratch_shapes=[
                    total_scratch,
                    pltpu.VMEM((columns // LANES, (steps + 1) * loads, LANES), F32),
                    history_scratch,
                ],
                compiler_params=params(12),
                cost_estimate=cost(3),
                name="far_next",
            )(lag_counts, lag_offset, tail, kernels, *arrived, *swapped)
            output = spread(block - 1, output, solved, chunks)
        received = [partials[0]] + trade_each(partials[1:])
        solved, sent, *following = solve(
            received, own_incident[block], state, block == 0, block + 1 == blocks
        )
        if following:
            rounded, state = following
    return spread(blocks - 1, output, solved, trade_each([sent] * (sources - 1)))


def solution(mesh):
    return jax.shard_map(
        local,
        mesh=mesh,
        in_specs=(
            P(None, None, "tgt"),
            P(None, None, "src"),
            P(None, "src", "tgt"),
            P("tgt", "src", None),
            P("tgt", "src"),
            P(None, "tgt", None),
            P("tgt", None),
        ),
        out_specs=P(None, None, "tgt"),
        check_vma=False,
    )
```
